128 devices in a mesh: expert: 16 (over x, z), tensor: 8 (over y, core).
Axes of the slice: x: 4, y: 4, z: 4, core: 2. Of those that a mesh axis runs over, the one named last changes fastest.
Arguments:
- layer_input: bfloat16 [8192, 2048], P('expert'), may hold values from -6 to 6
- attn_gain: float32 [2048], replicated, may hold values from 0.5 to 1.5
- w_query: bfloat16 [2048, 3072], P(None, 'tensor'), may hold values from -0.125 to 0.125
- w_kv_down: bfloat16 [2048, 576], replicated, may hold values from -0.125 to 0.125
- kv_gain: float32 [512], replicated, may hold values from 0.5 to 1.5
- w_kv_up: bfloat16 [512, 4096], P(None, 'tensor'), may hold values from -0.25 to 0.25
- w_out: bfloat16 [2048, 2048], P('tensor'), may hold values from -0.5 to 0.5
- ffn_gain: float32 [2048], replicated, may hold values from 0.5 to 1.5
- w_router: bfloat16 [2048, 32], replicated, may hold values from -0.0625 to 0.0625
- routes: int32 [8192, 6], P('expert'), may hold values from 0 to 31, all different within a row; in each aligned block of 512 rows (0 to 511, 512 to 1023, ...) at most 128 rows name the same one
- expert_gate: bfloat16 [32, 2048, 1408], P('expert', None, 'tensor'), may hold values from -0.125 to 0.125
- expert_up_projection: bfloat16 [32, 2048, 1408], P('expert', None, 'tensor'), may hold values from -0.125 to 0.125
- expert_down: bfloat16 [32, 1408, 2048], P('expert', 'tensor'), may hold values from -0.15625 to 0.15625
- shared_gate: bfloat16 [2048, 2816], P(None, 'tensor'), may hold values from -0.125 to 0.125
- shared_up: bfloat16 [2048, 2816], P(None, 'tensor'), may hold values from -0.125 to 0.125
- shared_down: bfloat16 [2816, 2048], P('tensor'), may hold values from -0.109375 to 0.109375
- cotangent: bfloat16 [8192, 2048], P(('expert', 'tensor')), may hold values from -6 to 6
Outputs:
- output: bfloat16 [8192, 2048], P(('expert', 'tensor'))
- grad_input: float32 [8192, 2048], P(('expert', 'tensor'))
- grad_attn_gain: float32 [2048], replicated
- grad_w_query: float32 [2048, 3072], P(None, 'tensor')
- grad_w_kv_down: float32 [2048, 576], replicated
- grad_kv_gain: float32 [512], replicated
- grad_w_kv_up: float32 [512, 4096], P(None, 'tensor')
- grad_w_out: float32 [2048, 2048], P('tensor')
- grad_ffn_gain: float32 [2048], replicated
- grad_w_router: float32 [2048, 32], replicated
- grad_expert_gate: float32 [32, 2048, 1408], P('expert', None, 'tensor')
- grad_expert_up: float32 [32, 2048, 1408], P('expert', None, 'tensor')
- grad_expert_down: float32 [32, 1408, 2048], P('expert', 'tensor')
- grad_shared_gate: float32 [2048, 2816], P(None, 'tensor')
- grad_shared_up: float32 [2048, 2816], P(None, 'tensor')
- grad_shared_down: float32 [2816, 2048], P('tensor')
The draws below stay inside these ranges and needn't reach their ends.
Inputs may be any that keep to these rules, and one draw needn't show every extreme that they name: `routes`: each row names 6 different experts. Among the 512 rows of one sequence no expert is named by more than 128 rows, a bound that some block reaches; every expert is named somewhere.
All inputs are finite; a program needn't handle non-finite values.
Results may differ from the reference program's by a relative error of at most 0.025.
Values may be sent and summed in bfloat16 or wider, within the bound.
No kernel may reach another device: no remote copies, remote signals or barrier semaphores. Data moves between devices by JAX's collectives and lax.ppermute only.
A program may use at most 384 MiB of HBM per device.

```python
import math
import jax
import jax.numpy as jnp
import numpy as np
from jax import lax

D = 2048
HEADS = 16
NOPE = 128
ROPE = 64
VDIM = 128
KV_RANK = 512
FF = 1408
SFF = 2816
TOP = 6
LEN = 512
EXPERTS = 32
TOKENS = 8192
CAP = 128
N_EXPERT = 16
N_TENSOR = 8


def levels(stream_key, shape, cuts, smallest, top_value):
    level = 1.0
    for dim, shards_of in cuts:
        steps = jax.random.uniform(jax.random.fold_in(jax.random.fold_in(stream_key, 6), dim), (shards_of,), jnp.float32, smallest / len(cuts), top_value / len(cuts))
        level = level * jnp.repeat(jnp.exp(steps), shape[dim] // shards_of).reshape((-1,) + (1,) * (len(shape) - 1 - dim))
    return level


def assign_block(stream_key, own, number, rows, amount, top, limit, slope):
    order = jax.random.permutation(stream_key, amount)
    heavy_load, ordinary = load_shares(amount, rows * top, limit, slope, True), load_shares(amount, rows * top, limit, slope, False)
    places = jnp.arange(amount)

    def named(sizes, turn):
        used = int((sizes > 0).sum())
        fixed = max(1, used // 4)
        moved = fixed + (places - fixed + turn * (used - fixed)) % max(1, amount - fixed)
        return jnp.zeros((amount,), jnp.int32).at[order[jnp.where(places < fixed, places, moved)]].set(jnp.asarray(sizes, jnp.int32))

    sizes = jnp.where(number % 4 == 0, named(heavy_load, number // 4), named(ordinary, number - number // 4 - 1))
    mixed = jax.random.permutation(jax.random.fold_in(own, 3), amount)
    giver, taker = mixed[0:amount // 2 * 2:2], mixed[1:amount // 2 * 2:2]
    room = jnp.minimum(sizes[giver] - 1, limit - sizes[taker]) // 2
    room = jnp.where((giver == order[0]) | (taker == order[0]) | (sizes[taker] == 0), 0, jnp.maximum(room, 0))
    moved = jax.random.randint(jax.random.fold_in(own, 4), (amount // 2,), 0, 1 << 20) % (room + 1)
    sizes = sizes.at[giver].add(-moved).at[taker].add(moved)
    labels = jnp.searchsorted(jnp.cumsum(sizes), jnp.arange(rows * top), side="right").astype(jnp.int32)
    listing = labels.reshape(top, rows).T
    listing = listing[jax.random.permutation(jax.random.fold_in(own, 1), rows)]
    turn = jax.random.randint(jax.random.fold_in(own, 2), (rows, 1), 0, top)
    return jnp.take_along_axis(listing, (jnp.arange(top)[None, :] + turn) % top, axis=1)


def load_shares(count, total, limit, skew, full):
    weights = [(1 << 20) // math.isqrt(grade ** skew) + 1 for grade in range(1, count + 1)]
    largest = limit if full else min(limit, max(-(-total // count), total * weights[0] // sum(weights)))
    least = 1 if total - largest >= count - 1 else 0
    given, spare = [largest] + [least] * (count - 1), total - largest - least * (count - 1)
    while spare > 0:
        free = [i for i in range(1, count) if given[i] < largest] or [i for i in range(1, count) if given[i] < limit]
        mass, left = sum([weights[i] for i in free]), spare
        for i in free:
            extra = min(limit - given[i], max(1, left * weights[i] // mass), spare)
            given[i] = given[i] + extra
            spare = spare - extra
    return np.array(given)


def centred(own_key, dims, scale, bound, shards=(), kind=jnp.bfloat16):
    factor_of = levels(own_key, dims, shards, -0.22, 0.18) if shards else 1.0
    values = jax.random.normal(own_key, dims, jnp.float32) * scale * factor_of
    return jnp.minimum(jnp.maximum(values, -bound), bound).astype(kind)


def setup_inputs(seed: int = 0) -> dict:
    streams_of = jax.random.split(jax.random.key(seed), 18)
    layer_input = centred(streams_of[0], (TOKENS, D), 1.0, 6.0, ((0, 16),))
    attn_gain = jnp.clip(1.0 + 0.1 * jax.random.normal(streams_of[1], (D,), jnp.float32), 0.5, 1.5)
    w_query = centred(streams_of[2], (D, HEADS * (NOPE + ROPE)), D ** -0.5, 0.125, ((1, 8),))
    w_kv_down = centred(streams_of[3], (D, KV_RANK + ROPE), D ** -0.5, 0.125)
    kv_gain = jnp.clip(1.0 + 0.1 * jax.random.normal(streams_of[4], (KV_RANK,), jnp.float32), 0.5, 1.5)
    w_kv_up = centred(streams_of[5], (KV_RANK, HEADS * (NOPE + VDIM)), KV_RANK ** -0.5, 0.25, ((1, 8),))
    w_out = centred(streams_of[6], (HEADS * VDIM, D), (HEADS * VDIM // 16) ** -0.5, 0.5, ((0, 8),))
    ffn_gain = jnp.clip(1.0 + 0.1 * jax.random.normal(streams_of[7], (D,), jnp.float32), 0.5, 1.5)
    w_router = centred(streams_of[8], (D, EXPERTS), (4 * D) ** -0.5, 0.0625)
    routes_keys = jax.random.split(jax.random.fold_in(streams_of[9], 1), TOKENS // LEN)
    routes_turns = jax.random.permutation(jax.random.fold_in(streams_of[9], 3), TOKENS // LEN)
    routes = jax.vmap(lambda own, number: assign_block(jax.random.fold_in(streams_of[9], 2), own, number, LEN, EXPERTS, TOP, CAP, 1))(routes_keys, routes_turns).reshape((TOKENS, TOP))
    expert_gate = centred(streams_of[10], (EXPERTS, D, FF), D ** -0.5, 0.125, ((0, 16), (2, 8)))
    expert_up_projection = centred(streams_of[11], (EXPERTS, D, FF), D ** -0.5, 0.125, ((0, 16), (2, 8)))
    expert_down = centred(streams_of[12], (EXPERTS, FF, D), FF ** -0.5, 0.15625, ((0, 16), (1, 8)))
    shared_gate = centred(streams_of[13], (D, SFF), D ** -0.5, 0.125, ((1, 8),))
    shared_up = centred(streams_of[14], (D, SFF), D ** -0.5, 0.125, ((1, 8),))
    shared_down = centred(streams_of[15], (SFF, D), SFF ** -0.5, 0.109375, ((0, 8),))
    cotangent = centred(streams_of[16], (TOKENS, D), 1.0, 6.0, ((0, 128),))
    return dict(layer_input=layer_input, attn_gain=attn_gain, w_query=w_query, w_kv_down=w_kv_down, kv_gain=kv_gain, w_kv_up=w_kv_up, w_out=w_out, ffn_gain=ffn_gain, w_router=w_router, routes=routes, expert_gate=expert_gate, expert_up_projection=expert_up_projection, expert_down=expert_down, shared_gate=shared_gate, shared_up=shared_up, shared_down=shared_down, cotangent=cotangent)


highest = lax.Precision.HIGHEST
epsilon = 1e-06
route_scale = 2.446
theta_base = 50000.0

@jax.custom_vjp
def low(v):
    return lax.optimization_barrier(v.astype(jnp.bfloat16)).astype(jnp.float32)

@jax.custom_vjp
def low_back(v):
    return v

def low_keep(v):
    return (low(v), None)

def low_pass(kept, grad):
    return (grad,)

def back_keep(v):
    return (v, None)

def back_low(kept, grad):
    return (low(grad),)
low.defvjp(low_keep, low_pass)
low_back.defvjp(back_keep, back_low)

def tables(length):
    half_width = ROPE // 2
    steps_float = jnp.arange(half_width, dtype=jnp.float32) * (2.0 / ROPE)
    frequency = jnp.exp(-jnp.log(theta_base) * steps_float)
    angles = jnp.arange(length, dtype=jnp.float32)[:, None] * frequency[None, :]
    return (jnp.cos(angles), jnp.sin(angles))

def rotate(values, cos_table, sin_table):
    half_width = ROPE // 2
    first_half = values[..., :half_width]
    second_half = values[..., half_width:]
    return jnp.concatenate([first_half * cos_table - second_half * sin_table, second_half * cos_table + first_half * sin_table], axis=-1)

def rms_norm(values, scales):
    return values * lax.rsqrt(lax.optimization_barrier(jnp.mean(values * values, axis=-1, keepdims=True)) + epsilon) * scales

def attend_sequence(sequence, attn_gain, w_query, w_kv_down, kv_gain, w_kv_up, w_out, cos_table, sin_table):
    length = sequence.shape[0]
    normed = low(rms_norm(sequence, attn_gain))
    query = low_back(jnp.dot(normed, w_query, precision=highest)).reshape(length, HEADS, NOPE + ROPE)
    query = low(jnp.concatenate([query[..., :NOPE], rotate(query[..., NOPE:], cos_table[:, None, :], sin_table[:, None, :])], axis=-1))
    compressed = low_back(jnp.dot(normed, w_kv_down, precision=highest))
    latent = low(rms_norm(compressed[:, :KV_RANK], kv_gain))
    key_rope = low(rotate(compressed[:, KV_RANK:], cos_table, sin_table))
    key_value = low(low_back(jnp.dot(latent, w_kv_up, precision=highest))).reshape(length, HEADS, NOPE + VDIM)
    scores = jnp.einsum('qhd,khd->hqk', query[..., :NOPE], key_value[..., :NOPE], precision=highest)
    scores = scores + jnp.einsum('qhd,kd->hqk', query[..., NOPE:], key_rope, precision=highest)
    scores = low_back(scores * (NOPE + ROPE) ** (-0.5))
    causal = jnp.arange(length)[:, None] >= jnp.arange(length)[None, :]
    scores = jnp.where(causal[None], scores, -1e+30)
    highest_score = lax.optimization_barrier(jnp.max(scores, axis=-1, keepdims=True))
    powered = jnp.exp(scores - highest_score)
    probs = low(powered / lax.optimization_barrier(jnp.sum(powered, axis=-1, keepdims=True)))
    heads_out = low(low_back(jnp.einsum('hqk,khd->qhd', probs, key_value[..., NOPE:], precision=highest)))
    return low_back(jnp.dot(heads_out.reshape(length, HEADS * VDIM), w_out, precision=highest))

def expert_block(row_block, gate_weight, up_weight, down_weight):
    count = row_block.shape[0]
    width = FF // N_TENSOR
    spread = low_back(jnp.broadcast_to(row_block[:, None, :], (count, N_TENSOR, D)))
    gate_value = low_back(jnp.einsum('rjd,djf->rjf', spread, gate_weight.reshape(D, N_TENSOR, width), precision=highest))
    up_value = low_back(jnp.einsum('rjd,djf->rjf', spread, up_weight.reshape(D, N_TENSOR, width), precision=highest))
    hidden = low(jax.nn.silu(gate_value) * up_value)
    partial_out = low(low_back(jnp.einsum('rjf,jfd->rjd', hidden, down_weight.reshape(N_TENSOR, width, D), precision=highest)))
    return lax.optimization_barrier(jnp.sum(partial_out, axis=1))

def slot_index(routes):
    chosen = (routes[:, :, None] == jnp.arange(EXPERTS, dtype=jnp.int32)[None, None, :]).astype(jnp.int32)
    counts = lax.optimization_barrier(jnp.sum(chosen, axis=1)).astype(jnp.int32).reshape(N_EXPERT, LEN, EXPERTS)
    before = (jnp.cumsum(counts, axis=1).astype(jnp.int32) - counts).reshape(TOKENS, EXPERTS)
    position = jnp.take_along_axis(before, routes, axis=1).astype(jnp.int32)
    source = (jnp.arange(TOKENS, dtype=jnp.int32) // LEN)[:, None]
    return (source * CAP + position).astype(jnp.int32)

def reference(layer_input, attn_gain, w_query, w_kv_down, kv_gain, w_kv_up, w_out, ffn_gain, w_router, routes, expert_gate, expert_up_projection, expert_down, shared_gate, shared_up, shared_down, cotangent):
    slots = slot_index(routes)
    cos_table, sin_table = tables(LEN)

    def forward_pass(input_full, attention_gain_full, query_weight_full, key_value_down_full, key_value_gain_full, key_value_up_full, output_weight_full, feedforward_gain_full, router_weight_full, expert_gate_full, expert_up_full, expert_down_full, shared_gate_full, shared_up_full, shared_down_full):
        sequences = input_full.reshape(N_EXPERT, LEN, D)
        one_sequence = jax.checkpoint(lambda sequence: attend_sequence(sequence, attention_gain_full, query_weight_full, key_value_down_full, key_value_gain_full, key_value_up_full, output_weight_full, cos_table, sin_table))
        attended = lax.map(one_sequence, sequences).reshape(TOKENS, D)
        residual = input_full + attended
        normed = low(rms_norm(residual, feedforward_gain_full))
        logits = low_back(jnp.dot(normed, router_weight_full, precision=highest))
        sigmoid_all = jax.nn.sigmoid(logits)
        selected = jnp.take_along_axis(sigmoid_all, routes, axis=1)
        gates = route_scale * selected / lax.optimization_barrier(jnp.sum(selected, axis=1, keepdims=True))
        holding_area = jnp.zeros((EXPERTS, N_EXPERT * CAP, D), jnp.float32)
        holding_area = holding_area.at[routes, slots].set(jnp.broadcast_to(normed[:, None, :], (TOKENS, TOP, D)))
        single_expert = jax.checkpoint(lambda operands: expert_block(operands[0], operands[1], operands[2], operands[3]))
        expert_output_rows = lax.map(single_expert, (holding_area, expert_gate_full, expert_up_full, expert_down_full))
        gathered = expert_output_rows[routes, slots]
        routed = lax.optimization_barrier(jnp.sum(gates[:, :, None] * gathered, axis=1))
        shared_gate_value = low_back(jnp.dot(normed, shared_gate_full, precision=highest))
        shared_up_value = low_back(jnp.dot(normed, shared_up_full, precision=highest))
        shared_act = low(jax.nn.silu(shared_gate_value) * shared_up_value)
        shared_result = low_back(jnp.dot(shared_act, shared_down_full, precision=highest))
        return residual + routed + shared_result
    floats = (layer_input.astype(jnp.float32), attn_gain.astype(jnp.float32), w_query.astype(jnp.float32), w_kv_down.astype(jnp.float32), kv_gain.astype(jnp.float32), w_kv_up.astype(jnp.float32), w_out.astype(jnp.float32), ffn_gain.astype(jnp.float32), w_router.astype(jnp.float32), expert_gate.astype(jnp.float32), expert_up_projection.astype(jnp.float32), expert_down.astype(jnp.float32), shared_gate.astype(jnp.float32), shared_up.astype(jnp.float32), shared_down.astype(jnp.float32))
    result, pullback = jax.vjp(forward_pass, *floats)
    grads = pullback(cotangent.astype(jnp.float32))
    return (result.astype(jnp.bfloat16), grads[0], grads[1], grads[2], grads[3], grads[4], grads[5], grads[6], grads[7], grads[8], grads[9], grads[10], grads[11], grads[12], grads[13], grads[14])
```

```python
import jax
import jax.numpy as jnp
from jax import lax
from jax.experimental import pallas as pl
from jax.experimental.pallas import tpu as pltpu
from jax.sharding import Mesh, PartitionSpec as P

D = 2048
NOPE = 128
ROPE = 64
VDIM = 128
KV_RANK = 512
TOP = 6
RANKS = 16
RINGS = 4
CORES = 2

epsilon = 1e-06
route_scale = 2.446
theta_base = 50000.0

EXPERT = ("x", "z")
GROUP = ("y", "core")
SWAP = [(0, 1), (1, 0)]
PAIRS = [(0, 1), (1, 0), (2, 3), (3, 2)]
OPPOSITE = [(0, 2), (2, 0), (1, 3), (3, 1)]
CROSS = [(1, 2), (2, 1), (3, 0), (0, 3)]


def after(x, *finished):
    return lax.optimization_barrier((x, *finished))[0]


def gather_rows(x):
    return lax.all_gather(x, GROUP, axis=0, tiled=True)


def gather_rows_directly(x, first_core):
    copies = jnp.broadcast_to(x[None], (RINGS, *x.shape))
    mine = lax.all_to_all(copies, "y", 0, 0, tiled=True)
    other = lax.ppermute(mine, "core", SWAP)
    first, second = jnp.where(first_core, mine, other), jnp.where(first_core, other, mine)
    return jnp.stack([first, second], axis=1).reshape(-1, x.shape[1])


def by_core(x, first_core):
    tiles = x.reshape(RINGS, CORES, x.shape[0] // (RINGS * CORES), x.shape[1])
    kept = jnp.where(first_core, tiles[:, 0], tiles[:, 1])
    given = jnp.where(first_core, tiles[:, 1], tiles[:, 0])
    return kept.reshape(-1, x.shape[1]), given.reshape(-1, x.shape[1])


def sum_rows(kept, given):
    other = lax.ppermute(given.astype(jnp.bfloat16), "core", SWAP)
    both = (kept.astype(jnp.float32) + other.astype(jnp.float32)).astype(jnp.bfloat16)
    tiles = both.reshape(RINGS, both.shape[0] // RINGS, both.shape[1])
    return lax.all_to_all(tiles, "y", 0, 0, tiled=True)


def sum_rows_directly(kept, given):
    other = lax.ppermute(given.astype(jnp.bfloat16), "core", SWAP)
    both = (kept.astype(jnp.float32) + other.astype(jnp.float32)).astype(jnp.bfloat16)
    tiles = both.reshape(RINGS, both.shape[0] // RINGS, both.shape[1])
    y = lax.axis_index("y")
    total = lax.dynamic_index_in_dim(tiles, y, 0, keepdims=False).astype(jnp.float32)
    for pairs in (PAIRS, CROSS, OPPOSITE):
        place = jnp.array([b for _, b in sorted(pairs)], jnp.int32)[y]
        tile = lax.dynamic_index_in_dim(tiles, place, 0, keepdims=False)
        total = total + lax.ppermute(tile, "y", pairs).astype(jnp.float32)
    return total


def total_of(tiles):
    return jnp.sum(tiles.astype(jnp.float32), axis=0)


def sum_ranks(x):
    tiles = lax.all_to_all(x, EXPERT, 0, 0, tiled=True)
    total = jnp.sum(tiles.astype(jnp.float32), axis=0).astype(jnp.bfloat16)
    return lax.all_to_all(jnp.broadcast_to(total[None], x.shape), EXPERT, 0, 0, tiled=True)


def angles_of(places):
    half_width = ROPE // 2
    steps_float = jnp.arange(half_width, dtype=jnp.float32) * (2.0 / ROPE)
    frequency = jnp.exp(-jnp.log(theta_base) * steps_float)
    angles = places.astype(jnp.float32)[:, None] * frequency[None, :]
    return (jnp.cos(angles), jnp.sin(angles))


def rotate(values, cos_table, sin_table):
    half_width = ROPE // 2
    first_half = values[..., :half_width]
    second_half = values[..., half_width:]
    return jnp.concatenate(
        [
            first_half * cos_table - second_half * sin_table,
            second_half * cos_table + first_half * sin_table,
        ],
        axis=-1,
    )


def rotate_back(upstream, cos_table, sin_table):
    half_width = ROPE // 2
    first_half = upstream[..., :half_width]
    second_half = upstream[..., half_width:]
    return jnp.concatenate(
        [
            first_half * cos_table + second_half * sin_table,
            second_half * cos_table - first_half * sin_table,
        ],
        axis=-1,
    )


def matmul(left, right):
    return jnp.dot(left, right, preferred_element_type=jnp.float32)


def matmul_tn(left, right):
    return lax.dot_general(
        left, right, (((0,), (0,)), ((), ())), preferred_element_type=jnp.float32
    )


def matmul_nt(left, right):
    return lax.dot_general(
        left, right, (((1,), (1,)), ((), ())), preferred_element_type=jnp.float32
    )


def norm_forward(values, scales):
    factor = lax.rsqrt(jnp.mean(values * values, axis=-1, keepdims=True) + epsilon)
    return (values * factor * scales, factor)


def norm_backward(values, factor, scales, upstream):
    scaled = upstream * scales
    cubed = factor * factor * factor
    d_values = factor * scaled - values * cubed * jnp.mean(scaled * values, axis=-1, keepdims=True)
    return (d_values, jnp.sum(upstream * values * factor, axis=0))


def split_float(v):
    high = v.astype(jnp.bfloat16)
    low = (v - high.astype(jnp.float32)).astype(jnp.bfloat16)
    return high, low


def to_owners(x):
    return lax.all_to_all(
        x.reshape(RANKS, x.shape[0] // RANKS, x.shape[1]), EXPERT, 0, 0, tiled=True
    ).reshape(x.shape)


HIDDEN = 176
TILE = 256
WIDTH = 512
LOW = 64
LONG = 100_000_000_000
SHORT = 18_000_000_000
VMEM_BYTES = 60 * 1024 * 1024


def dot_nt(left, right):
    return lax.dot_general(
        left, right, (((1,), (1,)), ((), ())), preferred_element_type=jnp.float32
    )


def dot_tn(left, right):
    return lax.dot_general(
        left, right, (((0,), (0,)), ((), ())), preferred_element_type=jnp.float32
    )


def hidden_loop(first, last, carry, step):
    return lax.fori_loop(
        first, last, lambda i, c: step(pl.multiple_of(i * TILE, TILE), TILE, c), carry
    )


def dispatch_kernel(map_ref, rows_ref, tail_ref, out):
    def some(j, carry):
        columns = pl.ds(pl.multiple_of(j * WIDTH, WIDTH), WIDTH)
        out[:, columns] = dot_tn(map_ref[...], rows_ref[:, columns]).astype(jnp.bfloat16)
        return carry

    lax.fori_loop(0, D // WIDTH, some, 0)
    out[:, D:] = dot_tn(map_ref[...], tail_ref[...]).astype(jnp.bfloat16)


def dispatch(slot_map, rows, tail):
    slots, width = slot_map.shape[1], rows.shape[1] + tail.shape[1]
    return pl.pallas_call(
        dispatch_kernel,
        out_shape=jax.ShapeDtypeStruct((slots, width), jnp.bfloat16),
        in_specs=[pl.BlockSpec(memory_space=pltpu.VMEM)] * 3,
        out_specs=pl.BlockSpec(memory_space=pltpu.VMEM),
        compiler_params=pltpu.CompilerParams(vmem_limit_bytes=VMEM_BYTES),
        cost_estimate=pl.CostEstimate(
            flops=2 * slots * slot_map.shape[0] * width, bytes_accessed=8 << 20, transcendentals=0
        ),
        name="dispatch",
    )(slot_map, rows, tail)


def shared_kernel(
    core,
    rows_ref,
    cot_ref,
    w_gate,
    w_up,
    w_down,
    gate_grads,
    up_grads,
    down_grads,
    act,
    kept,
    given,
    sgate,
    sup,
):
    block = rows_ref.shape[0] // (RINGS * CORES)
    gate_value = dot_nt(rows_ref[...], w_gate[...])
    up_value = dot_nt(rows_ref[...], w_up[...])
    back = dot_nt(cot_ref[...], w_down[...])
    sigma = jax.nn.sigmoid(gate_value)
    swish = gate_value * sigma
    act[...] = (swish * up_value).astype(jnp.bfloat16)
    slope = sigma * (1.0 + gate_value * (1.0 - sigma))
    sgate[...] = (back * up_value * slope).astype(jnp.bfloat16)
    sup[...] = (back * swish).astype(jnp.bfloat16)

    def some(j, carry):
        columns = pl.ds(pl.multiple_of(j * WIDTH, WIDTH), WIDTH)
        rows, cot = rows_ref[:, columns], cot_ref[:, columns]
        gate_grads[:, columns] = dot_tn(sgate[...], rows).astype(jnp.bfloat16)
        up_grads[:, columns] = dot_tn(sup[...], rows).astype(jnp.bfloat16)
        down_grads[:, columns] = dot_tn(act[...], cot).astype(jnp.bfloat16)
        value = jnp.dot(sgate[...], w_gate[:, columns], preferred_element_type=jnp.float32)
        value += jnp.dot(sup[...], w_up[:, columns], preferred_element_type=jnp.float32)
        for half in range(CORES):
            for target, chosen in ((kept, core[0] == half), (given, core[0] != half)):

                @pl.when(chosen)
                def _():
                    for chip in range(RINGS):
                        first = (chip * CORES + half) * block
                        target[chip * block : (chip + 1) * block, columns] = value[
                            first : first + block
                        ]

        return carry

    lax.fori_loop(0, D // WIDTH, some, 0)


def shared_experts(core, rows, cot, w_gate, w_up, w_down):
    length, width = rows.shape[0], w_gate.shape[0]
    half = jax.ShapeDtypeStruct((length // 2, D), jnp.float32)
    hidden = (length, width)
    vmem = pl.BlockSpec(memory_space=pltpu.VMEM)
    return pl.pallas_call(
        shared_kernel,
        out_shape=(jax.ShapeDtypeStruct((width, D), jnp.bfloat16),) * 3
        + (jax.ShapeDtypeStruct(hidden, jnp.bfloat16), half, half),
        in_specs=[pl.BlockSpec(memory_space=pltpu.SMEM)] + [vmem] * 5,
        out_specs=(vmem,) * 6,
        scratch_shapes=[pltpu.VMEM(hidden, jnp.bfloat16)] * 2,
        compiler_params=pltpu.CompilerParams(vmem_limit_bytes=VMEM_BYTES),
        cost_estimate=pl.CostEstimate(flops=SHORT, bytes_accessed=20 << 20, transcendentals=0),
        name="shared_experts",
    )(core, rows, cot, w_gate, w_up, w_down)


def kv_kernel(left, right, out):
    out[...] = jnp.dot(left[...], right[...], preferred_element_type=jnp.float32).astype(
        jnp.bfloat16
    )


def kv_product(left, right):
    vmem = pl.BlockSpec(memory_space=pltpu.VMEM)
    return pl.pallas_call(
        kv_kernel,
        out_shape=jax.ShapeDtypeStruct((left.shape[0], right.shape[1]), jnp.bfloat16),
        in_specs=[vmem] * 2,
        out_specs=vmem,
        compiler_params=pltpu.CompilerParams(vmem_limit_bytes=VMEM_BYTES),
        cost_estimate=pl.CostEstimate(flops=SHORT, bytes_accessed=4 << 20, transcendentals=0),
        name="kv_product",
    )(left, right)


def attention_kernel(
    core, query_ref, compressed_ref, x_ref, factor_ref, w_query, w_down, kept, given, gain
):
    block = x_ref.shape[0] // (RINGS * CORES)

    def some(j, carry):
        columns = pl.ds(pl.multiple_of(j * WIDTH, WIDTH), WIDTH)
        scaled = x_ref[:, columns].astype(jnp.float32) * factor_ref[...]
        value = dot_nt(query_ref[...], w_query[columns, :])
        value += jnp.dot(
            compressed_ref[...], w_down[:, columns], preferred_element_type=jnp.float32
        )
        gain[:, columns] = jnp.sum(value * scaled, axis=0, keepdims=True)
        value = value.astype(jnp.bfloat16)
        for half in range(CORES):
            for target, chosen in ((kept, core[0] == half), (given, core[0] != half)):

                @pl.when(chosen)
                def _():
                    for chip in range(RINGS):
                        first = (chip * CORES + half) * block
                        target[chip * block : (chip + 1) * block, columns] = value[
                            first : first + block
                        ]

        return carry

    lax.fori_loop(0, D // WIDTH, some, 0)


def attention_rows(core, query, compressed, x, factor, w_query, w_down):
    half = jax.ShapeDtypeStruct((x.shape[0] // 2, D), jnp.bfloat16)
    vmem = pl.BlockSpec(memory_space=pltpu.VMEM)
    return pl.pallas_call(
        attention_kernel,
        out_shape=(half, half, jax.ShapeDtypeStruct((1, D), jnp.float32)),
        in_specs=[pl.BlockSpec(memory_space=pltpu.SMEM)] + [vmem] * 6,
        out_specs=(vmem,) * 3,
        compiler_params=pltpu.CompilerParams(vmem_limit_bytes=VMEM_BYTES),
        cost_estimate=pl.CostEstimate(flops=LONG, bytes_accessed=10 << 20, transcendentals=0),
        name="attention_rows",
    )(core, query, compressed, x, factor, w_query, w_down)


def expert_kernel(*refs):
    expert, x_hbm, y_hbm = refs[:3]
    blocks = refs[3:11]
    back, gate_out, up_out, act_out = refs[11:15]
    x_ref, y_ref, w_gate, w_up, w_down, sems = refs[15:]
    total = w_gate.shape[0]
    copies = [
        pltpu.make_async_copy(x_hbm, x_ref, sems.at[0]),
        pltpu.make_async_copy(y_hbm, y_ref, sems.at[1]),
    ]
    for i, block in enumerate(blocks):
        rows = pl.ds(i * HIDDEN, HIDDEN)
        for m, w in enumerate((w_gate, w_up, w_down)):
            copies.append(
                pltpu.make_async_copy(
                    block.at[pl.ds(m * HIDDEN, HIDDEN)], w.at[rows], sems.at[2 + 3 * i + m]
                )
            )
    for copy in copies:
        copy.start()
    half = 2 + len(copies[2:]) // 2
    for copy in copies[:half]:
        copy.wait()
    lanes = lax.broadcasted_iota(jnp.int32, (x_ref.shape[0], 128), 1)
    high_lane, low_lane = lanes == expert[0], lanes == expert[0] + LOW
    tail = x_ref[:, D:].astype(jnp.float32)
    gate = jnp.sum(jnp.where(high_lane | low_lane, tail, 0.0), axis=-1, keepdims=True)

    def hidden(start, width, summed):
        rows = pl.ds(start, width)
        x = x_ref[:, :D]
        gate_value = dot_nt(x, w_gate[rows, :])
        up_value = dot_nt(x, w_up[rows, :])
        raw = dot_nt(y_ref[...], w_down[rows, :])
        sigma = jax.nn.sigmoid(gate_value)
        swish = gate_value * sigma
        act = swish * up_value
        summed = summed + jnp.sum(raw * act, axis=-1, keepdims=True)
        raw = raw * gate
        slope = sigma * (1.0 + gate_value * (1.0 - sigma))
        gate_out[:, rows] = (raw * up_value * slope).astype(jnp.bfloat16)
        up_out[:, rows] = (raw * swish).astype(jnp.bfloat16)
        act_out[:, rows] = (act * gate).astype(jnp.bfloat16)
        return summed

    ready = (total // 2) // TILE
    whole = total // TILE
    summed = hidden_loop(0, ready, jnp.zeros((x_ref.shape[0], 1), jnp.float32), hidden)
    for copy in copies[half:]:
        copy.wait()
    summed = hidden_loop(ready, whole, summed, hidden)
    if total % TILE:
        summed = hidden(whole * TILE, total % TILE, summed)
    high = summed.astype(jnp.bfloat16).astype(jnp.float32)
    back[:, D:] = jnp.where(
        high_lane, high, jnp.where(low_lane, summed - high, 0.0)
    ).astype(jnp.bfloat16)

    def inward(j, carry):
        columns = pl.ds(pl.multiple_of(j * WIDTH, WIDTH), WIDTH)
        value = jnp.dot(gate_out[...], w_gate[:, columns], preferred_element_type=jnp.float32)
        value += jnp.dot(up_out[...], w_up[:, columns], preferred_element_type=jnp.float32)
        back[:, columns] = value.astype(jnp.bfloat16)
        return carry

    lax.fori_loop(0, D // WIDTH, inward, 0)


def expert_rows(expert, x, g_y, blocks):
    slots = x.shape[0]
    total = HIDDEN * len(blocks)
    bf16 = jnp.bfloat16
    anywhere = pl.BlockSpec(memory_space=pl.ANY)
    vmem = pl.BlockSpec(memory_space=pltpu.VMEM)
    return pl.pallas_call(
        expert_kernel,
        out_shape=(jax.ShapeDtypeStruct(x.shape, bf16),)
        + (jax.ShapeDtypeStruct((slots, total), bf16),) * 3,
        in_specs=[pl.BlockSpec(memory_space=pltpu.SMEM)] + [anywhere] * (2 + len(blocks)),
        out_specs=(vmem,) * 4,
        scratch_shapes=[
            pltpu.VMEM(x.shape, bf16),
            pltpu.VMEM((slots, D), bf16),
            pltpu.VMEM((total, D), bf16),
            pltpu.VMEM((total, D), bf16),
            pltpu.VMEM((total, D), bf16),
            pltpu.SemaphoreType.DMA((2 + 3 * len(blocks),)),
        ],
        compiler_params=pltpu.CompilerParams(vmem_limit_bytes=VMEM_BYTES),
        cost_estimate=pl.CostEstimate(
            flops=10 * slots * total * D, bytes_accessed=28 << 20, transcendentals=slots * total
        ),
        name="expert_rows",
    )(expert, x, g_y, *blocks)


def expert_weights_kernel(*refs):
    x_ref, y_ref, gate_ref, up_ref, act_ref = refs[:5]
    blocks = refs[5:13]
    out, places = refs[13], refs[14:19]
    w_down, holds, sems = refs[19], refs[20:23], refs[23]
    total = gate_ref.shape[1]
    loads = []
    for i, block in enumerate(blocks):
        loads.append(
            pltpu.make_async_copy(
                block.at[pl.ds(2 * HIDDEN, HIDDEN)],
                w_down.at[pl.ds(i * HIDDEN, HIDDEN)],
                sems.at[i],
            )
        )
        loads[-1].start()
    copies = []
    for m, (left, right) in enumerate(((gate_ref, x_ref), (up_ref, x_ref), (act_ref, y_ref))):

        def hidden(start, width, carry):
            rows = pl.ds(start, width)
            holds[m][rows, :] = dot_tn(left[:, rows], right[:, :D]).astype(jnp.bfloat16)
            return carry

        hidden_loop(0, total // TILE, 0, hidden)
        if total % TILE:
            hidden(total // TILE * TILE, total % TILE, 0)
        for i in range(len(blocks)):
            first = m + 3 * max(i - RINGS, 0)
            place = places[min(i, RINGS)].at[pl.ds(first * HIDDEN, HIDDEN)]
            source = holds[m].at[pl.ds(i * HIDDEN, HIDDEN)]
            copies.append(
                pltpu.make_async_copy(source, place, sems.at[len(blocks) * (m + 1) + i])
            )
            copies[-1].start()
    for load in loads:
        load.wait()

    def outward(j, carry):
        columns = pl.ds(pl.multiple_of(j * WIDTH, WIDTH), WIDTH)
        value = jnp.dot(act_ref[...], w_down[:, columns], preferred_element_type=jnp.float32)
        out[:, columns] = value.astype(jnp.bfloat16)
        return carry

    lax.fori_loop(0, D // WIDTH, outward, 0)
    for copy in copies:
        copy.wait()


def expert_weights(x, g_y, gate, up, act, blocks):
    slots, total = gate.shape
    bf16 = jnp.bfloat16
    anywhere = pl.BlockSpec(memory_space=pl.ANY)
    vmem = pl.BlockSpec(memory_space=pltpu.VMEM)
    sizes = (3 * HIDDEN,) * RINGS + (3 * HIDDEN * RINGS,)
    return pl.pallas_call(
        expert_weights_kernel,
        out_shape=(jax.ShapeDtypeStruct((slots, D), bf16),)
        + tuple(jax.ShapeDtypeStruct((size, D), bf16) for size in sizes),
        in_specs=[vmem] * 5 + [anywhere] * len(blocks),
        out_specs=(vmem,) + (anywhere,) * 5,
        scratch_shapes=[pltpu.VMEM((total, D), bf16)] * 4
        + [pltpu.SemaphoreType.DMA((4 * len(blocks),))],
        compiler_params=pltpu.CompilerParams(vmem_limit_bytes=VMEM_BYTES),
        cost_estimate=pl.CostEstimate(
            flops=LONG, bytes_accessed=34 << 20, transcendentals=0
        ),
        name="expert_weights",
    )(x, g_y, gate, up, act, *blocks)


def shards(
    layer_input,
    attn_gain,
    w_query,
    w_kv_down,
    kv_gain,
    w_kv_up,
    w_out,
    ffn_gain,
    w_router,
    routes,
    expert_gate,
    expert_up_projection,
    expert_down,
    shared_gate,
    shared_up,
    shared_down,
    cotangent,
):
    length = layer_input.shape[0]
    rows = length // (RINGS * CORES)
    y, core = lax.axis_index("y"), lax.axis_index("core")
    qk_width = NOPE + ROPE
    heads_here = w_query.shape[1] // qk_width
    score_scale = qk_width ** (-0.5)
    experts_total = w_router.shape[1]
    first_core = core == 0
    second_expert = y >= RINGS // 2

    def block_of(expert):
        parts = (
            jnp.swapaxes(expert_gate, 1, 2),
            jnp.swapaxes(expert_up_projection, 1, 2),
            expert_down,
        )
        return jnp.concatenate(
            [lax.dynamic_index_in_dim(part, expert, 0, keepdims=False) for part in parts], axis=0
        )

    same = second_expert.astype(jnp.int32)
    same_block, other_block = block_of(same), block_of(1 - same)
    weights = [
        same_block,
        lax.ppermute(same_block, "y", PAIRS),
        lax.ppermute(other_block, "y", CROSS),
    ]

    places = jnp.arange(length, dtype=jnp.int32)
    own_start = (y * CORES + core) * rows
    cot_all = gather_rows(cotangent)
    cot_rows = cotangent.astype(jnp.float32)

    def own(table):
        return lax.dynamic_slice_in_dim(table, own_start, rows, 0)

    def parts_of(table):
        return by_core(table, first_core)

    expert_ids = jnp.arange(experts_total, dtype=jnp.int32)
    picked = jnp.zeros((length, experts_total), jnp.float32)
    for route in range(TOP):
        picked = picked + (routes[:, route : route + 1] == expert_ids[None, :]).astype(jnp.float32)
    earlier = (places[:, None] > places[None, :]).astype(jnp.bfloat16)
    before = matmul(earlier, picked.astype(jnp.bfloat16))
    share = 128 // RINGS
    quarter = (y % 2) * CORES + core
    slots = jnp.arange(RANKS * share, dtype=jnp.int32)
    expert_of_slot = (experts_total // RANKS) * (slots // share) + same
    spread = (expert_ids[:, None] == expert_of_slot[None, :]).astype(jnp.bfloat16)
    place_of = matmul((picked * (before + 1.0)).astype(jnp.bfloat16), spread)
    slot_number = (slots % share + share * quarter + 1).astype(jnp.float32)
    slot_map = (place_of == slot_number[None, :]).astype(jnp.bfloat16)
    slot_parts = parts_of(slot_map)
    g_y_sent = matmul_tn(slot_map, cot_all).astype(jnp.bfloat16)
    g_y = to_owners(g_y_sent)

    cos_table, sin_table = angles_of(places)
    input_full = layer_input.astype(jnp.float32)
    normed_full, factor_one = norm_forward(input_full, attn_gain)
    normed_a = normed_full.astype(jnp.bfloat16)
    query_raw = matmul(normed_a, w_query).reshape(length, heads_here, qk_width)
    query_turned = rotate(query_raw[..., NOPE:], cos_table[:, None, :], sin_table[:, None, :])
    query = jnp.concatenate([query_raw[..., :NOPE], query_turned], axis=-1).astype(jnp.bfloat16)
    compressed = matmul(normed_a, w_kv_down)
    latent_raw = compressed[:, :KV_RANK]
    latent_normed, factor_kv = norm_forward(latent_raw, kv_gain)
    latent = latent_normed.astype(jnp.bfloat16)
    key_rope = rotate(compressed[:, KV_RANK:], cos_table, sin_table).astype(jnp.bfloat16)
    key_value = (
        matmul(latent, w_kv_up).astype(jnp.bfloat16).reshape(length, heads_here, NOPE + VDIM)
    )
    key_nope = key_value[..., :NOPE]
    values_all = key_value[..., NOPE:]
    causal = places[:, None] >= places[None, :]

    def scores_of(query):
        scores = jnp.einsum(
            "qhd,khd->hqk", query[..., :NOPE], key_nope, preferred_element_type=jnp.float32
        )
        scores = scores + jnp.einsum(
            "qhd,kd->hqk", query[..., NOPE:], key_rope, preferred_element_type=jnp.float32
        )
        return jnp.where(causal[None], scores * score_scale, -1e30)

    scores = scores_of(query)
    top_score = jnp.max(scores, axis=-1, keepdims=True)
    powered = jnp.exp(scores - top_score)
    total = jnp.sum(powered, axis=-1, keepdims=True)
    probs = (powered / total).astype(jnp.bfloat16)
    log_totals = top_score + jnp.log(total)
    heads_out = (
        jnp.einsum("hqk,khd->qhd", probs, values_all, preferred_element_type=jnp.float32)
        .astype(jnp.bfloat16)
        .reshape(length, heads_here * VDIM)
    )
    attn_kept, attn_given = parts_of(matmul(heads_out, w_out).astype(jnp.bfloat16))
    attended = sum_rows_directly(after(attn_kept, g_y_sent, *weights[1:]), attn_given)
    residual = own(input_full) + attended
    normed_two, factor_two = norm_forward(residual, ffn_gain)
    normed_rows = normed_two.astype(jnp.bfloat16)
    normed_f = gather_rows(normed_rows)
    weights.append(lax.ppermute(after(other_block, normed_f), "y", OPPOSITE))

    sigmoid_all = jax.nn.sigmoid(matmul(normed_f, w_router))
    selected = sigmoid_all * picked
    sel_total = jnp.sum(selected, axis=-1, keepdims=True)
    gates = route_scale * selected / sel_total
    high, low = split_float(gates)
    gap = jnp.zeros((length, LOW - experts_total), jnp.bfloat16)
    sent = dispatch(slot_map, normed_f, jnp.concatenate([high, gap, low, gap], axis=1))
    arrived = to_owners(after(sent, g_y))

    core_index = core.reshape(1).astype(jnp.int32)
    *grads_shared, shared_act, kept_back, given_back = shared_experts(
        core_index,
        after(normed_f, sent),
        cot_all,
        jnp.swapaxes(shared_gate, 0, 1),
        jnp.swapaxes(shared_up, 0, 1),
        shared_down,
    )

    shared_back = (kept_back, given_back)

    arrived = after(arrived, *shared_back)
    last = after(weights[-1], arrived)
    weights = weights + [lax.ppermute(w, "core", SWAP) for w in (*weights[:-1], last)]
    expert_here = 2 * lax.axis_index("x") * 4 + 2 * lax.axis_index("z") + same
    back, g_gate, g_up, act = expert_rows(
        expert_here.reshape(1).astype(jnp.int32), arrived, g_y, weights
    )
    out, *block_grads = expert_weights(
        arrived, g_y, g_gate, g_up, act, weights
    )
    back = after(to_owners(back), *block_grads)

    taken_grads = lax.ppermute(block_grads[RINGS], "core", SWAP)
    taken_grads = [taken_grads[3 * HIDDEN * r : 3 * HIDDEN * (r + 1)] for r in range(RINGS)]
    grads_sent = [
        (mine.astype(jnp.float32) + taken.astype(jnp.float32)).astype(jnp.bfloat16)
        for mine, taken in zip(block_grads[1:RINGS], taken_grads[1:])
    ]

    summed = sum_rows_directly(
        *(
            matmul(a, back) + jnp.pad(b, ((0, 0), (0, 128)))
            for a, b in zip(slot_parts, shared_back)
        )
    )
    g_gate_rows = summed[:, D : D + experts_total] + summed[:, D + LOW : D + LOW + experts_total]

    sigma_rows, picked_rows, total_rows = own(sigmoid_all), own(picked), own(sel_total)
    sel_rows = sigma_rows * picked_rows
    grad_sel = route_scale * (
        g_gate_rows / total_rows
        - jnp.sum(g_gate_rows * sel_rows, axis=-1, keepdims=True) / (total_rows * total_rows)
    )
    grad_logits = (grad_sel * picked_rows * sigma_rows * (1.0 - sigma_rows)).astype(jnp.bfloat16)
    grad_w_router = matmul_tn(grad_logits, normed_rows)
    grad_normed = summed[:, :D] + matmul_nt(grad_logits, w_router)
    grad_from_norm, grad_ffn_gain = norm_backward(residual, factor_two, ffn_gain, grad_normed)
    grad_residual = cot_rows + grad_from_norm
    grad_residual_low = grad_residual.astype(jnp.bfloat16)
    grad_attended = gather_rows(grad_residual_low)
    returned = to_owners(after(out, grad_residual_low))

    grad_attended, *grads_sent = lax.optimization_barrier((grad_attended, *grads_sent))
    grads_got = [lax.ppermute(g, "y", pairs) for g, pairs in zip(grads_sent, (PAIRS, CROSS))]
    grad_w_out = matmul_tn(heads_out, grad_attended).astype(jnp.bfloat16)

    grad_heads = (
        matmul_nt(grad_attended, w_out).astype(jnp.bfloat16).reshape(length, heads_here, VDIM)
    )
    probs_full = jnp.exp(scores_of(query) - log_totals)
    grad_probs = jnp.einsum(
        "qhd,khd->hqk", grad_heads, values_all, preferred_element_type=jnp.float32
    )
    grad_scores = (
        probs_full * (grad_probs - jnp.sum(grad_probs * probs_full, axis=-1, keepdims=True))
    ).astype(jnp.bfloat16)
    grad_query_nope = (
        jnp.einsum("hqk,khd->qhd", grad_scores, key_nope, preferred_element_type=jnp.float32)
        * score_scale
    )
    grad_query_rope = (
        jnp.einsum("hqk,kd->qhd", grad_scores, key_rope, preferred_element_type=jnp.float32)
        * score_scale
    )
    grad_key_nope = (
        jnp.einsum(
            "hqk,qhd->khd", grad_scores, query[..., :NOPE], preferred_element_type=jnp.float32
        )
        * score_scale
    )
    grad_key_rope = (
        jnp.einsum(
            "hqk,qhd->kd", grad_scores, query[..., NOPE:], preferred_element_type=jnp.float32
        )
        * score_scale
    )
    grad_values = jnp.einsum(
        "hqk,qhd->khd",
        probs_full.astype(jnp.bfloat16),
        grad_heads,
        preferred_element_type=jnp.float32,
    )
    grad_query_back = rotate_back(
        grad_query_rope, cos_table[:, None, :], sin_table[:, None, :]
    )
    grad_query = (
        jnp.concatenate([grad_query_nope, grad_query_back], axis=-1)
        .astype(jnp.bfloat16)
        .reshape(length, heads_here * qk_width)
    )
    returned = after(returned, grad_query)
    act_parts = parts_of(shared_act)
    routed_and_shared = sum_rows_directly(
        *(matmul(a, returned) + matmul(b, shared_down) for a, b in zip(slot_parts, act_parts))
    )
    output = (residual + routed_and_shared).astype(jnp.bfloat16)
    grad_w_query = matmul_tn(normed_a, grad_query).astype(jnp.bfloat16)
    grad_key_value = (
        jnp.concatenate([grad_key_nope, grad_values], axis=-1)
        .astype(jnp.bfloat16)
        .reshape(length, heads_here * (NOPE + VDIM))
    )
    grad_w_kv_up = matmul_tn(latent, grad_key_value).astype(jnp.bfloat16)
    grad_latent_normed = matmul_nt(grad_key_value, w_kv_up)
    grad_latent, grad_kv_gain = norm_backward(latent_raw, factor_kv, kv_gain, grad_latent_normed)
    grad_rope_part = rotate_back(grad_key_rope, cos_table, sin_table)
    grad_compressed = jnp.concatenate([grad_latent, grad_rope_part], axis=-1).astype(jnp.bfloat16)
    local_grads = (grad_w_out, grad_w_query, grad_w_kv_up, *grads_shared)
    grad_w_out, grad_w_query, grad_w_kv_up, *grads_shared = lax.psum(local_grads, EXPERT)
    kept, given, grad_attn_gain = attention_rows(
        core_index,
        grad_query,
        grad_compressed,
        layer_input,
        factor_one,
        w_query,
        jnp.swapaxes(w_kv_down, 0, 1),
    )

    parts = RINGS * CORES
    kv_share = grad_compressed.shape[1] // parts
    columns = D // parts
    gains = jnp.concatenate(
        [
            grad_attn_gain.reshape(parts, columns),
            grad_ffn_gain.reshape(parts, columns),
            grad_kv_gain.reshape(parts, KV_RANK // parts),
        ],
        axis=1,
    )
    gains = jnp.pad(gains, ((0, 0), (0, 16 * length // 2 - gains.shape[1])))
    bundle = jnp.concatenate(
        [
            jnp.swapaxes(grad_compressed, 0, 1).reshape(parts, kv_share, length),
            jnp.swapaxes(grad_w_router.reshape(experts_total, parts, columns), 0, 1)
            .reshape(parts, experts_total * columns // length, length)
            .astype(jnp.bfloat16),
            gains.reshape(parts, 8, length).astype(jnp.bfloat16),
        ],
        axis=1,
    )
    bundle = after(bundle, returned, *local_grads)
    bundle = jnp.sum(
        lax.all_to_all(bundle, GROUP, 0, 0, tiled=True).astype(jnp.float32), axis=0
    ).astype(jnp.bfloat16)
    grads_got.append(lax.ppermute(after(grads_sent[2], bundle), "y", OPPOSITE))
    grad_normed_one = sum_rows_directly(kept, given)
    grad_from_first, _ = norm_backward(
        own(input_full), own(factor_one), attn_gain, grad_normed_one
    )
    grad_input = grad_residual + grad_from_first
    kv_slice = kv_product(bundle[:kv_share], normed_a)
    other_rows = bundle[kv_share:].reshape(-1, D)
    replicated = jnp.concatenate(
        [kv_slice, other_rows, jnp.zeros((80 - kv_share - other_rows.shape[0], D), jnp.bfloat16)],
        axis=0,
    )
    replicated = jnp.swapaxes(replicated.reshape(80, RANKS, D // RANKS), 0, 1)
    replicated = sum_ranks(replicated)
    def by_expert(m):
        part = slice(m * HIDDEN, (m + 1) * HIDDEN)
        ours = block_grads[0][part].astype(jnp.float32) + taken_grads[0][part].astype(jnp.float32)
        ours = ours + grads_got[0][part].astype(jnp.float32)
        others = grads_got[1][part].astype(jnp.float32) + grads_got[2][part].astype(jnp.float32)
        return jnp.stack(
            [jnp.where(second_expert, others, ours), jnp.where(second_expert, ours, others)]
        )

    expert_grads = [by_expert(m) for m in range(3)]
    replicated = gather_rows_directly(replicated.reshape(RANKS * 80, D // RANKS), first_core)
    replicated = replicated.reshape(parts, RANKS, 80, D // RANKS)
    replicated = jnp.swapaxes(replicated, 1, 2).reshape(parts, 80, D).astype(jnp.float32)
    grad_w_kv_down = jnp.swapaxes(replicated[:, :kv_share].reshape(-1, D), 0, 1)
    others = replicated[:, kv_share:]
    router_rows = experts_total * columns // D
    grad_w_router = (
        jnp.swapaxes(others[:, :router_rows].reshape(parts, experts_total, columns), 0, 1)
        .reshape(experts_total, D)
        .T
    )
    gains = others[:, router_rows]
    grad_attn_gain = gains[:, :columns].reshape(D)
    grad_ffn_gain = gains[:, columns : 2 * columns].reshape(D)
    grad_kv_gain = gains[:, 2 * columns : 2 * columns + KV_RANK // parts].reshape(KV_RANK)
    grads_shared = [grad.astype(jnp.float32) for grad in grads_shared]
    return (
        output,
        grad_input,
        grad_attn_gain,
        grad_w_query.astype(jnp.float32),
        grad_w_kv_down,
        grad_kv_gain,
        grad_w_kv_up.astype(jnp.float32),
        grad_w_out.astype(jnp.float32),
        grad_ffn_gain,
        grad_w_router,
        jnp.swapaxes(expert_grads[0], 1, 2),
        jnp.swapaxes(expert_grads[1], 1, 2),
        expert_grads[2],
        grads_shared[0].T,
        grads_shared[1].T,
        grads_shared[2],
    )


def solution(mesh):
    split = Mesh(mesh.devices.reshape(4, 4, RINGS, CORES), ("x", "z", "y", "core"))
    return jax.shard_map(
        shards,
        mesh=split,
        in_specs=(
            P(EXPERT, None),
            P(),
            P(None, GROUP),
            P(),
            P(),
            P(None, GROUP),
            P(GROUP, None),
            P(),
            P(),
            P(EXPERT, None),
            P(EXPERT, None, GROUP),
            P(EXPERT, None, GROUP),
            P(EXPERT, GROUP, None),
            P(None, GROUP),
            P(None, GROUP),
            P(GROUP, None),
            P(("x", "z", "y", "core"), None),
        ),
        out_specs=(
            P(("x", "z", "y", "core"), None),
            P(("x", "z", "y", "core"), None),
            P(),
            P(None, GROUP),
            P(),
            P(),
            P(None, GROUP),
            P(GROUP, None),
            P(),
            P(),
            P(EXPERT, None, GROUP),
            P(EXPERT, None, GROUP),
            P(EXPERT, GROUP, None),
            P(None, GROUP),
            P(None, GROUP),
            P(GROUP, None),
        ),
        check_vma=False,
    )
```

```python
import jax
import jax.numpy as jnp
from jax import lax
from jax.experimental import pallas as pl
from jax.experimental.pallas import tpu as pltpu
from jax.sharding import Mesh, PartitionSpec as P

D = 2048
NOPE = 128
ROPE = 64
VDIM = 128
KV_RANK = 512
TOP = 6
RANKS = 16
RINGS = 4
CORES = 2

epsilon = 1e-06
route_scale = 2.446
theta_base = 50000.0

EXPERT = ("x", "z")
GROUP = ("y", "core")
SWAP = [(0, 1), (1, 0)]
PAIRS = [(0, 1), (1, 0), (2, 3), (3, 2)]
OPPOSITE = [(0, 2), (2, 0), (1, 3), (3, 1)]
CROSS = [(1, 2), (2, 1), (3, 0), (0, 3)]


def after(x, *finished):
    return lax.optimization_barrier((x, *finished))[0]


def gather_rows(x):
    return lax.all_gather(x, GROUP, axis=0, tiled=True)


def gather_rows_directly(x, first_core, beside):
    copies = jnp.broadcast_to(x[None], (RINGS, *x.shape))
    mine = lax.all_to_all(copies, "y", 0, 0, tiled=True)
    mine = after(mine, *beside)
    other = lax.ppermute(mine, "core", SWAP)
    first, second = jnp.where(first_core, mine, other), jnp.where(first_core, other, mine)
    return jnp.stack([first, second], axis=1).reshape(-1, x.shape[1])


def as_unit(work, always):
    shapes = jax.eval_shape(work)
    return lax.cond(
        always, work, lambda: jax.tree.map(lambda a: jnp.zeros(a.shape, a.dtype), shapes)
    )


def by_core(x, first_core):
    tiles = x.reshape(RINGS, CORES, x.shape[0] // (RINGS * CORES), x.shape[1])
    kept = jnp.where(first_core, tiles[:, 0], tiles[:, 1])
    given = jnp.where(first_core, tiles[:, 1], tiles[:, 0])
    return kept.reshape(-1, x.shape[1]), given.reshape(-1, x.shape[1])


def sum_rows(kept, given):
    other = lax.ppermute(given.astype(jnp.bfloat16), "core", SWAP)
    both = (kept.astype(jnp.float32) + other.astype(jnp.float32)).astype(jnp.bfloat16)
    tiles = both.reshape(RINGS, both.shape[0] // RINGS, both.shape[1])
    return lax.all_to_all(tiles, "y", 0, 0, tiled=True)


def sum_rows_directly(kept, given):
    other = lax.ppermute(given.astype(jnp.bfloat16), "core", SWAP)
    both = (kept.astype(jnp.float32) + other.astype(jnp.float32)).astype(jnp.bfloat16)
    tiles = both.reshape(RINGS, both.shape[0] // RINGS, both.shape[1])
    y = lax.axis_index("y")
    total = lax.dynamic_index_in_dim(tiles, y, 0, keepdims=False).astype(jnp.float32)
    for pairs in (PAIRS, CROSS, OPPOSITE):
        place = jnp.array([b for _, b in sorted(pairs)], jnp.int32)[y]
        tile = lax.dynamic_index_in_dim(tiles, place, 0, keepdims=False)
        total = total + lax.ppermute(tile, "y", pairs).astype(jnp.float32)
    return total


def total_of(tiles):
    return jnp.sum(tiles.astype(jnp.float32), axis=0)


def sum_ranks(x):
    tiles = lax.all_to_all(x, EXPERT, 0, 0, tiled=True)
    total = jnp.sum(tiles.astype(jnp.float32), axis=0).astype(jnp.bfloat16)
    return lax.all_to_all(jnp.broadcast_to(total[None], x.shape), EXPERT, 0, 0, tiled=True)


def angles_of(places):
    half_width = ROPE // 2
    steps_float = jnp.arange(half_width, dtype=jnp.float32) * (2.0 / ROPE)
    frequency = jnp.exp(-jnp.log(theta_base) * steps_float)
    angles = places.astype(jnp.float32)[:, None] * frequency[None, :]
    return (jnp.cos(angles), jnp.sin(angles))


def rotate(values, cos_table, sin_table):
    half_width = ROPE // 2
    first_half = values[..., :half_width]
    second_half = values[..., half_width:]
    return jnp.concatenate(
        [
            first_half * cos_table - second_half * sin_table,
            second_half * cos_table + first_half * sin_table,
        ],
        axis=-1,
    )


def rotate_back(upstream, cos_table, sin_table):
    half_width = ROPE // 2
    first_half = upstream[..., :half_width]
    second_half = upstream[..., half_width:]
    return jnp.concatenate(
        [
            first_half * cos_table + second_half * sin_table,
            second_half * cos_table - first_half * sin_table,
        ],
        axis=-1,
    )


def matmul(left, right):
    return jnp.dot(left, right, preferred_element_type=jnp.float32)


def matmul_tn(left, right):
    return lax.dot_general(
        left, right, (((0,), (0,)), ((), ())), preferred_element_type=jnp.float32
    )


def matmul_nt(left, right):
    return lax.dot_general(
        left, right, (((1,), (1,)), ((), ())), preferred_element_type=jnp.float32
    )


def norm_forward(values, scales):
    factor = lax.rsqrt(jnp.mean(values * values, axis=-1, keepdims=True) + epsilon)
    return (values * factor * scales, factor)


def norm_backward(values, factor, scales, upstream):
    scaled = upstream * scales
    cubed = factor * factor * factor
    d_values = factor * scaled - values * cubed * jnp.mean(scaled * values, axis=-1, keepdims=True)
    return (d_values, jnp.sum(upstream * values * factor, axis=0))


def split_float(v):
    high = v.astype(jnp.bfloat16)
    low = (v - high.astype(jnp.float32)).astype(jnp.bfloat16)
    return high, low


def to_owners(x):
    return lax.all_to_all(
        x.reshape(RANKS, x.shape[0] // RANKS, x.shape[1]), EXPERT, 0, 0, tiled=True
    ).reshape(x.shape)


HIDDEN = 176
TILE = 256
WIDTH = 512
LOW = 64
LONG = 100_000_000_000
SHORT = 18_000_000_000
VMEM_BYTES = 60 * 1024 * 1024


def dot_nt(left, right):
    return lax.dot_general(
        left, right, (((1,), (1,)), ((), ())), preferred_element_type=jnp.float32
    )


def dot_tn(left, right):
    return lax.dot_general(
        left, right, (((0,), (0,)), ((), ())), preferred_element_type=jnp.float32
    )


def hidden_loop(first, last, carry, step):
    return lax.fori_loop(
        first, last, lambda i, c: step(pl.multiple_of(i * TILE, TILE), TILE, c), carry
    )


def dispatch_kernel(map_ref, rows_ref, tail_ref, out):
    def some(j, carry):
        columns = pl.ds(pl.multiple_of(j * WIDTH, WIDTH), WIDTH)
        out[:, columns] = dot_tn(map_ref[...], rows_ref[:, columns]).astype(jnp.bfloat16)
        return carry

    lax.fori_loop(0, D // WIDTH, some, 0)
    out[:, D:] = dot_tn(map_ref[...], tail_ref[...]).astype(jnp.bfloat16)


def dispatch(slot_map, rows, tail):
    slots, width = slot_map.shape[1], rows.shape[1] + tail.shape[1]
    return pl.pallas_call(
        dispatch_kernel,
        out_shape=jax.ShapeDtypeStruct((slots, width), jnp.bfloat16),
        in_specs=[pl.BlockSpec(memory_space=pltpu.VMEM)] * 3,
        out_specs=pl.BlockSpec(memory_space=pltpu.VMEM),
        compiler_params=pltpu.CompilerParams(vmem_limit_bytes=VMEM_BYTES),
        cost_estimate=pl.CostEstimate(
            flops=2 * slots * slot_map.shape[0] * width, bytes_accessed=8 << 20, transcendentals=0
        ),
        name="dispatch",
    )(slot_map, rows, tail)


def shared_kernel(
    core,
    rows_ref,
    cot_ref,
    w_gate,
    w_up,
    w_down,
    gate_grads,
    up_grads,
    down_grads,
    act,
    kept,
    given,
    sgate,
    sup,
):
    block = rows_ref.shape[0] // (RINGS * CORES)
    gate_value = dot_nt(rows_ref[...], w_gate[...])
    up_value = dot_nt(rows_ref[...], w_up[...])
    back = dot_nt(cot_ref[...], w_down[...])
    sigma = jax.nn.sigmoid(gate_value)
    swish = gate_value * sigma
    act[...] = (swish * up_value).astype(jnp.bfloat16)
    slope = sigma * (1.0 + gate_value * (1.0 - sigma))
    sgate[...] = (back * up_value * slope).astype(jnp.bfloat16)
    sup[...] = (back * swish).astype(jnp.bfloat16)

    def some(j, carry):
        columns = pl.ds(pl.multiple_of(j * WIDTH, WIDTH), WIDTH)
        rows, cot = rows_ref[:, columns], cot_ref[:, columns]
        gate_grads[:, columns] = dot_tn(sgate[...], rows).astype(jnp.bfloat16)
        up_grads[:, columns] = dot_tn(sup[...], rows).astype(jnp.bfloat16)
        down_grads[:, columns] = dot_tn(act[...], cot).astype(jnp.bfloat16)
        value = jnp.dot(sgate[...], w_gate[:, columns], preferred_element_type=jnp.float32)
        value += jnp.dot(sup[...], w_up[:, columns], preferred_element_type=jnp.float32)
        for half in range(CORES):
            for target, chosen in ((kept, core[0] == half), (given, core[0] != half)):

                @pl.when(chosen)
                def _():
                    for chip in range(RINGS):
                        first = (chip * CORES + half) * block
                        target[chip * block : (chip + 1) * block, columns] = value[
                            first : first + block
                        ]

        return carry

    lax.fori_loop(0, D // WIDTH, some, 0)


def shared_experts(core, rows, cot, w_gate, w_up, w_down):
    length, width = rows.shape[0], w_gate.shape[0]
    half = jax.ShapeDtypeStruct((length // 2, D), jnp.float32)
    hidden = (length, width)
    vmem = pl.BlockSpec(memory_space=pltpu.VMEM)
    return pl.pallas_call(
        shared_kernel,
        out_shape=(jax.ShapeDtypeStruct((width, D), jnp.bfloat16),) * 3
        + (jax.ShapeDtypeStruct(hidden, jnp.bfloat16), half, half),
        in_specs=[pl.BlockSpec(memory_space=pltpu.SMEM)] + [vmem] * 5,
        out_specs=(vmem,) * 6,
        scratch_shapes=[pltpu.VMEM(hidden, jnp.bfloat16)] * 2,
        compiler_params=pltpu.CompilerParams(vmem_limit_bytes=VMEM_BYTES),
        cost_estimate=pl.CostEstimate(flops=SHORT, bytes_accessed=20 << 20, transcendentals=0),
        name="shared_experts",
    )(core, rows, cot, w_gate, w_up, w_down)


def expert_outputs_kernel(same, own, taken_hbm, pair, cross, far, *refs):
    outs, taken, sem = refs[:3], refs[3], refs[4]
    copy = pltpu.make_async_copy(taken_hbm.at[pl.ds(0, 3 * HIDDEN)], taken, sem)
    copy.start()
    copy.wait()
    for m, out in enumerate(outs):
        rows = slice(m * HIDDEN, (m + 1) * HIDDEN)
        ours = own[rows, :].astype(jnp.float32) + taken[rows, :].astype(jnp.float32)
        ours += pair[rows, :].astype(jnp.float32)
        others = cross[rows, :].astype(jnp.float32) + far[rows, :].astype(jnp.float32)
        out[same[0]] = ours
        out[1 - same[0]] = others


def expert_outputs(same, own, taken, pair, cross, far):
    vmem = pl.BlockSpec(memory_space=pltpu.VMEM)
    first = pl.BlockSpec(memory_space=pl.ANY)
    return pl.pallas_call(
        expert_outputs_kernel,
        out_shape=(jax.ShapeDtypeStruct((CORES, HIDDEN, D), jnp.float32),) * 3,
        in_specs=[pl.BlockSpec(memory_space=pltpu.SMEM), vmem, first] + [vmem] * 3,
        out_specs=(vmem,) * 3,
        scratch_shapes=[pltpu.VMEM((3 * HIDDEN, D), jnp.bfloat16), pltpu.SemaphoreType.DMA],
        compiler_params=pltpu.CompilerParams(vmem_limit_bytes=VMEM_BYTES),
        cost_estimate=pl.CostEstimate(flops=0, bytes_accessed=20 << 20, transcendentals=0),
        name="expert_outputs",
    )(same, own, taken, pair, cross, far)


def kv_kernel(left, right, out):
    out[...] = jnp.dot(left[...], right[...], preferred_element_type=jnp.float32).astype(
        jnp.bfloat16
    )


def kv_product(left, right):
    vmem = pl.BlockSpec(memory_space=pltpu.VMEM)
    return pl.pallas_call(
        kv_kernel,
        out_shape=jax.ShapeDtypeStruct((left.shape[0], right.shape[1]), jnp.bfloat16),
        in_specs=[vmem] * 2,
        out_specs=vmem,
        compiler_params=pltpu.CompilerParams(vmem_limit_bytes=VMEM_BYTES),
        cost_estimate=pl.CostEstimate(flops=LONG, bytes_accessed=4 << 20, transcendentals=0),
        name="kv_product",
    )(left, right)


def attention_kernel(
    core, query_ref, compressed_ref, x_ref, factor_ref, w_query, w_down, kept, given, gain
):
    block = x_ref.shape[0] // (RINGS * CORES)

    def some(j, carry):
        columns = pl.ds(pl.multiple_of(j * WIDTH, WIDTH), WIDTH)
        scaled = x_ref[:, columns].astype(jnp.float32) * factor_ref[...]
        value = dot_nt(query_ref[...], w_query[columns, :])
        value += jnp.dot(
            compressed_ref[...], w_down[:, columns], preferred_element_type=jnp.float32
        )
        gain[:, columns] = jnp.sum(value * scaled, axis=0, keepdims=True)
        value = value.astype(jnp.bfloat16)
        for half in range(CORES):
            for target, chosen in ((kept, core[0] == half), (given, core[0] != half)):

                @pl.when(chosen)
                def _():
                    for chip in range(RINGS):
                        first = (chip * CORES + half) * block
                        target[chip * block : (chip + 1) * block, columns] = value[
                            first : first + block
                        ]

        return carry

    lax.fori_loop(0, D // WIDTH, some, 0)


def attention_rows(core, query, compressed, x, factor, w_query, w_down):
    half = jax.ShapeDtypeStruct((x.shape[0] // 2, D), jnp.bfloat16)
    vmem = pl.BlockSpec(memory_space=pltpu.VMEM)
    return pl.pallas_call(
        attention_kernel,
        out_shape=(half, half, jax.ShapeDtypeStruct((1, D), jnp.float32)),
        in_specs=[pl.BlockSpec(memory_space=pltpu.SMEM)] + [vmem] * 6,
        out_specs=(vmem,) * 3,
        compiler_params=pltpu.CompilerParams(vmem_limit_bytes=VMEM_BYTES),
        cost_estimate=pl.CostEstimate(flops=LONG, bytes_accessed=10 << 20, transcendentals=0),
        name="attention_rows",
    )(core, query, compressed, x, factor, w_query, w_down)


def expert_kernel(*refs):
    expert, x_hbm, y_hbm = refs[:3]
    blocks = refs[3:11]
    back, gate_out, up_out, act_out = refs[11:15]
    x_ref, y_ref, w_gate, w_up, w_down, sems = refs[15:]
    total = w_gate.shape[0]
    copies = [
        pltpu.make_async_copy(x_hbm, x_ref, sems.at[0]),
        pltpu.make_async_copy(y_hbm, y_ref, sems.at[1]),
    ]
    for i, block in enumerate(blocks):
        rows = pl.ds(i * HIDDEN, HIDDEN)
        for m, w in enumerate((w_gate, w_up, w_down)):
            copies.append(
                pltpu.make_async_copy(
                    block.at[pl.ds(m * HIDDEN, HIDDEN)], w.at[rows], sems.at[2 + 3 * i + m]
                )
            )
    for copy in copies:
        copy.start()
    half = 2 + len(copies[2:]) // 2
    for copy in copies[:half]:
        copy.wait()
    lanes = lax.broadcasted_iota(jnp.int32, (x_ref.shape[0], 128), 1)
    high_lane, low_lane = lanes == expert[0], lanes == expert[0] + LOW
    tail = x_ref[:, D:].astype(jnp.float32)
    gate = jnp.sum(jnp.where(high_lane | low_lane, tail, 0.0), axis=-1, keepdims=True)

    def hidden(start, width, summed):
        rows = pl.ds(start, width)
        x = x_ref[:, :D]
        gate_value = dot_nt(x, w_gate[rows, :])
        up_value = dot_nt(x, w_up[rows, :])
        raw = dot_nt(y_ref[...], w_down[rows, :])
        sigma = jax.nn.sigmoid(gate_value)
        swish = gate_value * sigma
        act = swish * up_value
        summed = summed + jnp.sum(raw * act, axis=-1, keepdims=True)
        raw = raw * gate
        slope = sigma * (1.0 + gate_value * (1.0 - sigma))
        gate_out[:, rows] = (raw * up_value * slope).astype(jnp.bfloat16)
        up_out[:, rows] = (raw * swish).astype(jnp.bfloat16)
        act_out[:, rows] = (act * gate).astype(jnp.bfloat16)
        return summed

    ready = (total // 2) // TILE
    whole = total // TILE
    summed = hidden_loop(0, ready, jnp.zeros((x_ref.shape[0], 1), jnp.float32), hidden)
    for copy in copies[half:]:
        copy.wait()
    summed = hidden_loop(ready, whole, summed, hidden)
    if total % TILE:
        summed = hidden(whole * TILE, total % TILE, summed)
    high = summed.astype(jnp.bfloat16).astype(jnp.float32)
    back[:, D:] = jnp.where(
        high_lane, high, jnp.where(low_lane, summed - high, 0.0)
    ).astype(jnp.bfloat16)

    def inward(j, carry):
        columns = pl.ds(pl.multiple_of(j * WIDTH, WIDTH), WIDTH)
        value = jnp.dot(gate_out[...], w_gate[:, columns], preferred_element_type=jnp.float32)
        value += jnp.dot(up_out[...], w_up[:, columns], preferred_element_type=jnp.float32)
        back[:, columns] = value.astype(jnp.bfloat16)
        return carry

    lax.fori_loop(0, D // WIDTH, inward, 0)


def expert_rows(expert, x, g_y, blocks):
    slots = x.shape[0]
    total = HIDDEN * len(blocks)
    bf16 = jnp.bfloat16
    anywhere = pl.BlockSpec(memory_space=pl.ANY)
    vmem = pl.BlockSpec(memory_space=pltpu.VMEM)
    return pl.pallas_call(
        expert_kernel,
        out_shape=(jax.ShapeDtypeStruct(x.shape, bf16),)
        + (jax.ShapeDtypeStruct((slots, total), bf16),) * 3,
        in_specs=[pl.BlockSpec(memory_space=pltpu.SMEM)] + [anywhere] * (2 + len(blocks)),
        out_specs=(vmem,) * 4,
        scratch_shapes=[
            pltpu.VMEM(x.shape, bf16),
            pltpu.VMEM((slots, D), bf16),
            pltpu.VMEM((total, D), bf16),
            pltpu.VMEM((total, D), bf16),
            pltpu.VMEM((total, D), bf16),
            pltpu.SemaphoreType.DMA((2 + 3 * len(blocks),)),
        ],
        compiler_params=pltpu.CompilerParams(vmem_limit_bytes=VMEM_BYTES),
        cost_estimate=pl.CostEstimate(
            flops=10 * slots * total * D, bytes_accessed=28 << 20, transcendentals=slots * total
        ),
        name="expert_rows",
    )(expert, x, g_y, *blocks)


def expert_weights_kernel(*refs):
    x_ref, y_ref, gate_ref, up_ref, act_ref = refs[:5]
    blocks = refs[5:13]
    out, places = refs[13], refs[14:19]
    w_down, holds, sems = refs[19], refs[20:23], refs[23]
    total = gate_ref.shape[1]
    loads = []
    for i, block in enumerate(blocks):
        loads.append(
            pltpu.make_async_copy(
                block.at[pl.ds(2 * HIDDEN, HIDDEN)],
                w_down.at[pl.ds(i * HIDDEN, HIDDEN)],
                sems.at[i],
            )
        )
        loads[-1].start()
    copies = []
    for m, (left, right) in enumerate(((gate_ref, x_ref), (up_ref, x_ref), (act_ref, y_ref))):

        def hidden(start, width, carry):
            rows = pl.ds(start, width)
            holds[m][rows, :] = dot_tn(left[:, rows], right[:, :D]).astype(jnp.bfloat16)
            return carry

        hidden_loop(0, total // TILE, 0, hidden)
        if total % TILE:
            hidden(total // TILE * TILE, total % TILE, 0)
        for i in range(len(blocks)):
            first = m + 3 * max(i - RINGS, 0)
            place = places[min(i, RINGS)].at[pl.ds(first * HIDDEN, HIDDEN)]
            source = holds[m].at[pl.ds(i * HIDDEN, HIDDEN)]
            copies.append(
                pltpu.make_async_copy(source, place, sems.at[len(blocks) * (m + 1) + i])
            )
            copies[-1].start()
    for load in loads:
        load.wait()

    def outward(j, carry):
        columns = pl.ds(pl.multiple_of(j * WIDTH, WIDTH), WIDTH)
        value = jnp.dot(act_ref[...], w_down[:, columns], preferred_element_type=jnp.float32)
        out[:, columns] = value.astype(jnp.bfloat16)
        return carry

    lax.fori_loop(0, D // WIDTH, outward, 0)
    for copy in copies:
        copy.wait()


def expert_weights(x, g_y, gate, up, act, blocks):
    slots, total = gate.shape
    bf16 = jnp.bfloat16
    anywhere = pl.BlockSpec(memory_space=pl.ANY)
    vmem = pl.BlockSpec(memory_space=pltpu.VMEM)
    sizes = (3 * HIDDEN,) * RINGS + (3 * HIDDEN * RINGS,)
    return pl.pallas_call(
        expert_weights_kernel,
        out_shape=(jax.ShapeDtypeStruct((slots, D), bf16),)
        + tuple(jax.ShapeDtypeStruct((size, D), bf16) for size in sizes),
        in_specs=[vmem] * 5 + [anywhere] * len(blocks),
        out_specs=(vmem,) + (anywhere,) * 5,
        scratch_shapes=[pltpu.VMEM((total, D), bf16)] * 4
        + [pltpu.SemaphoreType.DMA((4 * len(blocks),))],
        compiler_params=pltpu.CompilerParams(vmem_limit_bytes=VMEM_BYTES),
        cost_estimate=pl.CostEstimate(
            flops=LONG, bytes_accessed=34 << 20, transcendentals=0
        ),
        name="expert_weights",
    )(x, g_y, gate, up, act, *blocks)


def shards(
    layer_input,
    attn_gain,
    w_query,
    w_kv_down,
    kv_gain,
    w_kv_up,
    w_out,
    ffn_gain,
    w_router,
    routes,
    expert_gate,
    expert_up_projection,
    expert_down,
    shared_gate,
    shared_up,
    shared_down,
    cotangent,
):
    length = layer_input.shape[0]
    rows = length // (RINGS * CORES)
    y, core = lax.axis_index("y"), lax.axis_index("core")
    qk_width = NOPE + ROPE
    heads_here = w_query.shape[1] // qk_width
    score_scale = qk_width ** (-0.5)
    experts_total = w_router.shape[1]
    first_core = core == 0
    second_expert = y >= RINGS // 2

    def block_of(expert):
        parts = (
            jnp.swapaxes(expert_gate, 1, 2),
            jnp.swapaxes(expert_up_projection, 1, 2),
            expert_down,
        )
        return jnp.concatenate(
            [lax.dynamic_index_in_dim(part, expert, 0, keepdims=False) for part in parts], axis=0
        )

    same = second_expert.astype(jnp.int32)
    same_block, other_block = block_of(same), block_of(1 - same)
    weights = [
        same_block,
        lax.ppermute(same_block, "y", PAIRS),
        lax.ppermute(other_block, "y", CROSS),
    ]

    places = jnp.arange(length, dtype=jnp.int32)
    own_start = (y * CORES + core) * rows
    cot_all = gather_rows(cotangent)
    cot_rows = cotangent.astype(jnp.float32)

    def own(table):
        return lax.dynamic_slice_in_dim(table, own_start, rows, 0)

    def parts_of(table):
        return by_core(table, first_core)

    expert_ids = jnp.arange(experts_total, dtype=jnp.int32)
    picked = jnp.zeros((length, experts_total), jnp.float32)
    for route in range(TOP):
        picked = picked + (routes[:, route : route + 1] == expert_ids[None, :]).astype(jnp.float32)
    earlier = (places[:, None] > places[None, :]).astype(jnp.bfloat16)
    before = matmul(earlier, picked.astype(jnp.bfloat16))
    share = 128 // RINGS
    quarter = (y % 2) * CORES + core
    slots = jnp.arange(RANKS * share, dtype=jnp.int32)
    expert_of_slot = (experts_total // RANKS) * (slots // share) + same
    spread = (expert_ids[:, None] == expert_of_slot[None, :]).astype(jnp.bfloat16)
    place_of = matmul((picked * (before + 1.0)).astype(jnp.bfloat16), spread)
    slot_number = (slots % share + share * quarter + 1).astype(jnp.float32)
    slot_map = (place_of == slot_number[None, :]).astype(jnp.bfloat16)
    slot_parts = parts_of(slot_map)
    g_y_sent = matmul_tn(slot_map, cot_all).astype(jnp.bfloat16)
    g_y = to_owners(g_y_sent)

    cos_table, sin_table = angles_of(places)
    input_full = layer_input.astype(jnp.float32)
    normed_full, factor_one = norm_forward(input_full, attn_gain)
    normed_a = normed_full.astype(jnp.bfloat16)
    query_raw = matmul(normed_a, w_query).reshape(length, heads_here, qk_width)
    query_turned = rotate(query_raw[..., NOPE:], cos_table[:, None, :], sin_table[:, None, :])
    query = jnp.concatenate([query_raw[..., :NOPE], query_turned], axis=-1).astype(jnp.bfloat16)
    compressed = matmul(normed_a, w_kv_down)
    latent_raw = compressed[:, :KV_RANK]
    latent_normed, factor_kv = norm_forward(latent_raw, kv_gain)
    latent = latent_normed.astype(jnp.bfloat16)
    key_rope = rotate(compressed[:, KV_RANK:], cos_table, sin_table).astype(jnp.bfloat16)
    key_value = (
        matmul(latent, w_kv_up).astype(jnp.bfloat16).reshape(length, heads_here, NOPE + VDIM)
    )
    key_nope = key_value[..., :NOPE]
    values_all = key_value[..., NOPE:]
    causal = places[:, None] >= places[None, :]

    def scores_of(query):
        scores = jnp.einsum(
            "qhd,khd->hqk", query[..., :NOPE], key_nope, preferred_element_type=jnp.float32
        )
        scores = scores + jnp.einsum(
            "qhd,kd->hqk", query[..., NOPE:], key_rope, preferred_element_type=jnp.float32
        )
        return jnp.where(causal[None], scores * score_scale, -1e30)

    scores = scores_of(query)
    top_score = jnp.max(scores, axis=-1, keepdims=True)
    powered = jnp.exp(scores - top_score)
    total = jnp.sum(powered, axis=-1, keepdims=True)
    probs = (powered / total).astype(jnp.bfloat16)
    log_totals = top_score + jnp.log(total)
    heads_out = (
        jnp.einsum("hqk,khd->qhd", probs, values_all, preferred_element_type=jnp.float32)
        .astype(jnp.bfloat16)
        .reshape(length, heads_here * VDIM)
    )
    attn_kept, attn_given = parts_of(matmul(heads_out, w_out).astype(jnp.bfloat16))
    attended = sum_rows_directly(after(attn_kept, g_y_sent, *weights[1:]), attn_given)
    residual = own(input_full) + attended
    normed_two, factor_two = norm_forward(residual, ffn_gain)
    normed_rows = normed_two.astype(jnp.bfloat16)
    normed_f = gather_rows(normed_rows)
    weights.append(lax.ppermute(after(other_block, normed_f), "y", OPPOSITE))

    sigmoid_all = jax.nn.sigmoid(matmul(normed_f, w_router))
    selected = sigmoid_all * picked
    sel_total = jnp.sum(selected, axis=-1, keepdims=True)
    gates = route_scale * selected / sel_total
    high, low = split_float(gates)
    gap = jnp.zeros((length, LOW - experts_total), jnp.bfloat16)
    sent = dispatch(slot_map, normed_f, jnp.concatenate([high, gap, low, gap], axis=1))
    arrived = to_owners(after(sent, g_y))

    core_index = core.reshape(1).astype(jnp.int32)
    *grads_shared, shared_act, kept_back, given_back = shared_experts(
        core_index,
        after(normed_f, sent),
        cot_all,
        jnp.swapaxes(shared_gate, 0, 1),
        jnp.swapaxes(shared_up, 0, 1),
        shared_down,
    )

    shared_back = (kept_back, given_back)

    arrived = after(arrived, *shared_back)
    last = after(weights[-1], arrived)
    weights = weights + [lax.ppermute(w, "core", SWAP) for w in (*weights[:-1], last)]
    expert_here = 2 * lax.axis_index("x") * 4 + 2 * lax.axis_index("z") + same
    back, g_gate, g_up, act = expert_rows(
        expert_here.reshape(1).astype(jnp.int32), arrived, g_y, weights
    )
    out, *block_grads = expert_weights(
        arrived, g_y, g_gate, g_up, act, weights
    )
    back = after(to_owners(back), *block_grads)

    taken_grads = lax.ppermute(block_grads[RINGS], "core", SWAP)
    grads_sent = [
        (
            block_grads[r].astype(jnp.float32)
            + taken_grads[3 * HIDDEN * r : 3 * HIDDEN * (r + 1)].astype(jnp.float32)
        ).astype(jnp.bfloat16)
        for r in range(1, RINGS)
    ]

    summed = sum_rows_directly(
        *(
            matmul(a, back) + jnp.pad(b, ((0, 0), (0, 128)))
            for a, b in zip(slot_parts, shared_back)
        )
    )
    g_gate_rows = summed[:, D : D + experts_total] + summed[:, D + LOW : D + LOW + experts_total]

    sigma_rows, picked_rows, total_rows = own(sigmoid_all), own(picked), own(sel_total)
    sel_rows = sigma_rows * picked_rows
    grad_sel = route_scale * (
        g_gate_rows / total_rows
        - jnp.sum(g_gate_rows * sel_rows, axis=-1, keepdims=True) / (total_rows * total_rows)
    )
    grad_logits = (grad_sel * picked_rows * sigma_rows * (1.0 - sigma_rows)).astype(jnp.bfloat16)
    grad_w_router = matmul_tn(grad_logits, normed_rows)
    grad_normed = summed[:, :D] + matmul_nt(grad_logits, w_router)
    grad_from_norm, grad_ffn_gain = norm_backward(residual, factor_two, ffn_gain, grad_normed)
    grad_residual = cot_rows + grad_from_norm
    grad_residual_low = grad_residual.astype(jnp.bfloat16)
    grad_attended = gather_rows(grad_residual_low)
    returned = to_owners(after(out, grad_residual_low))

    grad_w_out = matmul_tn(heads_out, grad_attended).astype(jnp.bfloat16)

    grad_heads = (
        matmul_nt(grad_attended, w_out).astype(jnp.bfloat16).reshape(length, heads_here, VDIM)
    )
    probs_full = jnp.exp(scores_of(query) - log_totals)
    grad_probs = jnp.einsum(
        "qhd,khd->hqk", grad_heads, values_all, preferred_element_type=jnp.float32
    )
    grad_scores = (
        probs_full * (grad_probs - jnp.sum(grad_probs * probs_full, axis=-1, keepdims=True))
    ).astype(jnp.bfloat16)
    grad_query_nope = (
        jnp.einsum("hqk,khd->qhd", grad_scores, key_nope, preferred_element_type=jnp.float32)
        * score_scale
    )
    grad_query_rope = (
        jnp.einsum("hqk,kd->qhd", grad_scores, key_rope, preferred_element_type=jnp.float32)
        * score_scale
    )
    grad_key_nope = (
        jnp.einsum(
            "hqk,qhd->khd", grad_scores, query[..., :NOPE], preferred_element_type=jnp.float32
        )
        * score_scale
    )
    grad_key_rope = (
        jnp.einsum(
            "hqk,qhd->kd", grad_scores, query[..., NOPE:], preferred_element_type=jnp.float32
        )
        * score_scale
    )
    grad_values = jnp.einsum(
        "hqk,qhd->khd",
        probs_full.astype(jnp.bfloat16),
        grad_heads,
        preferred_element_type=jnp.float32,
    )
    grad_query_back = rotate_back(
        grad_query_rope, cos_table[:, None, :], sin_table[:, None, :]
    )
    grad_query = (
        jnp.concatenate([grad_query_nope, grad_query_back], axis=-1)
        .astype(jnp.bfloat16)
        .reshape(length, heads_here * qk_width)
    )
    grad_w_query = matmul_tn(normed_a, grad_query).astype(jnp.bfloat16)
    grad_key_value = (
        jnp.concatenate([grad_key_nope, grad_values], axis=-1)
        .astype(jnp.bfloat16)
        .reshape(length, heads_here * (NOPE + VDIM))
    )
    grad_w_kv_up = matmul_tn(latent, grad_key_value).astype(jnp.bfloat16)
    grad_latent_normed = matmul_nt(grad_key_value, w_kv_up)
    grad_latent, grad_kv_gain = norm_backward(latent_raw, factor_kv, kv_gain, grad_latent_normed)
    grad_rope_part = rotate_back(grad_key_rope, cos_table, sin_table)
    grad_compressed = jnp.concatenate([grad_latent, grad_rope_part], axis=-1).astype(jnp.bfloat16)
    local_grads = (grad_w_out, grad_w_query, grad_w_kv_up, *grads_shared)
    grad_w_out, grad_w_query, grad_w_kv_up, *grads_shared = lax.psum(local_grads, EXPERT)
    kept, given, grad_attn_gain = attention_rows(
        core_index,
        grad_query,
        grad_compressed,
        layer_input,
        factor_one,
        w_query,
        jnp.swapaxes(w_kv_down, 0, 1),
    )

    parts = RINGS * CORES
    kv_share = grad_compressed.shape[1] // parts
    columns = D // parts
    gains = jnp.concatenate(
        [
            grad_attn_gain.reshape(parts, columns),
            grad_ffn_gain.reshape(parts, columns),
            grad_kv_gain.reshape(parts, KV_RANK // parts),
        ],
        axis=1,
    )
    gains = jnp.pad(gains, ((0, 0), (0, 16 * length // 2 - gains.shape[1])))
    bundle = jnp.concatenate(
        [
            jnp.swapaxes(grad_compressed, 0, 1).reshape(parts, kv_share, length),
            jnp.swapaxes(grad_w_router.reshape(experts_total, parts, columns), 0, 1)
            .reshape(parts, experts_total * columns // length, length)
            .astype(jnp.bfloat16),
            gains.reshape(parts, 8, length).astype(jnp.bfloat16),
        ],
        axis=1,
    )
    bundle = after(bundle, returned, *local_grads)

    def last_sums():
        tiles = lax.all_to_all(bundle, GROUP, 0, 0, tiled=True)
        slices = total_of(tiles).astype(jnp.bfloat16)
        pair_grads = lax.ppermute(grads_sent[0], "y", PAIRS)
        cross_grads = lax.ppermute(grads_sent[1], "y", CROSS)
        grad_normed_one = sum_rows_directly(kept, given)
        act_parts = parts_of(shared_act)
        routed_and_shared = sum_rows_directly(
            *(matmul(a, returned) + matmul(b, shared_down) for a, b in zip(slot_parts, act_parts))
        )
        output = (residual + routed_and_shared).astype(jnp.bfloat16)
        grad_from_first, _ = norm_backward(
            own(input_full), own(factor_one), attn_gain, grad_normed_one
        )
        grad_input = grad_residual + grad_from_first
        far_grads = lax.ppermute(
            after(grads_sent[2], slices), "y", OPPOSITE
        )
        kv_slice = kv_product(slices[:kv_share], normed_a)
        other_rows = slices[kv_share:].reshape(-1, D)
        rest = jnp.zeros((80 - kv_share - other_rows.shape[0], D), jnp.bfloat16)
        replicated = jnp.concatenate([kv_slice, other_rows, rest], axis=0)
        replicated = jnp.swapaxes(replicated.reshape(80, RANKS, D // RANKS), 0, 1)
        replicated = sum_ranks(replicated)
        expert_grads = expert_outputs(
            same.reshape(1), block_grads[0], taken_grads, pair_grads, cross_grads, far_grads
        )
        replicated = after(
            replicated, pair_grads, cross_grads, far_grads
        )
        replicated = gather_rows_directly(
            replicated.reshape(RANKS * 80, D // RANKS), first_core, expert_grads
        )
        return grad_input, replicated, output, expert_grads

    grad_input, replicated, output, expert_grads = as_unit(
        last_sums, routes[0, 0] >= 0
    )
    replicated = replicated.reshape(parts, RANKS, 80, D // RANKS)
    replicated = jnp.swapaxes(replicated, 1, 2).reshape(parts, 80, D).astype(jnp.float32)
    grad_w_kv_down = jnp.swapaxes(replicated[:, :kv_share].reshape(-1, D), 0, 1)
    others = replicated[:, kv_share:]
    router_rows = experts_total * columns // D
    grad_w_router = (
        jnp.swapaxes(others[:, :router_rows].reshape(parts, experts_total, columns), 0, 1)
        .reshape(experts_total, D)
        .T
    )
    gains = others[:, router_rows]
    grad_attn_gain = gains[:, :columns].reshape(D)
    grad_ffn_gain = gains[:, columns : 2 * columns].reshape(D)
    grad_kv_gain = gains[:, 2 * columns : 2 * columns + KV_RANK // parts].reshape(KV_RANK)
    grads_shared = [grad.astype(jnp.float32) for grad in grads_shared]
    return (
        output,
        grad_input,
        grad_attn_gain,
        grad_w_query.astype(jnp.float32),
        grad_w_kv_down,
        grad_kv_gain,
        grad_w_kv_up.astype(jnp.float32),
        grad_w_out.astype(jnp.float32),
        grad_ffn_gain,
        grad_w_router,
        jnp.swapaxes(expert_grads[0], 1, 2),
        jnp.swapaxes(expert_grads[1], 1, 2),
        expert_grads[2],
        grads_shared[0].T,
        grads_shared[1].T,
        grads_shared[2],
    )


def solution(mesh):
    split = Mesh(mesh.devices.reshape(4, 4, RINGS, CORES), ("x", "z", "y", "core"))
    return jax.shard_map(
        shards,
        mesh=split,
        in_specs=(
            P(EXPERT, None),
            P(),
            P(None, GROUP),
            P(),
            P(),
            P(None, GROUP),
            P(GROUP, None),
            P(),
            P(),
            P(EXPERT, None),
            P(EXPERT, None, GROUP),
            P(EXPERT, None, GROUP),
            P(EXPERT, GROUP, None),
            P(None, GROUP),
            P(None, GROUP),
            P(GROUP, None),
            P(("x", "z", "y", "core"), None),
        ),
        out_specs=(
            P(("x", "z", "y", "core"), None),
            P(("x", "z", "y", "core"), None),
            P(),
            P(None, GROUP),
            P(),
            P(),
            P(None, GROUP),
            P(GROUP, None),
            P(),
            P(),
            P(EXPERT, None, GROUP),
            P(EXPERT, None, GROUP),
            P(EXPERT, GROUP, None),
            P(None, GROUP),
            P(None, GROUP),
            P(GROUP, None),
        ),
        check_vma=False,
    )
```

```python
import jax
import jax.numpy as jnp
from jax import lax
from jax.experimental import pallas as pl
from jax.experimental.pallas import tpu as pltpu
from jax.sharding import Mesh, PartitionSpec as P

D = 2048
NOPE = 128
ROPE = 64
VDIM = 128
KV_RANK = 512
TOP = 6
RANKS = 16
RINGS = 4
CORES = 2

epsilon = 1e-06
route_scale = 2.446
theta_base = 50000.0

EXPERT = ("x", "z")
GROUP = ("y", "core")
SWAP = [(0, 1), (1, 0)]
PAIRS = [(0, 1), (1, 0), (2, 3), (3, 2)]
OPPOSITE = [(0, 2), (2, 0), (1, 3), (3, 1)]
CROSS = [(1, 2), (2, 1), (3, 0), (0, 3)]


def after(x, *finished):
    return lax.optimization_barrier((x, *finished))[0]


def gather_rows(x):
    return lax.all_gather(x, GROUP, axis=0, tiled=True)


def gather_rows_directly(x, first_core, beside):
    copies = jnp.broadcast_to(x[None], (RINGS, *x.shape))
    mine = lax.all_to_all(copies, "y", 0, 0, tiled=True)
    mine = after(mine, *beside)
    other = lax.ppermute(mine, "core", SWAP)
    first, second = jnp.where(first_core, mine, other), jnp.where(first_core, other, mine)
    return jnp.stack([first, second], axis=1).reshape(-1, x.shape[1])


def as_unit(work, always):
    shapes = jax.eval_shape(work)
    return lax.cond(
        always, work, lambda: jax.tree.map(lambda a: jnp.zeros(a.shape, a.dtype), shapes)
    )


def by_core(x, first_core):
    tiles = x.reshape(RINGS, CORES, x.shape[0] // (RINGS * CORES), x.shape[1])
    kept = jnp.where(first_core, tiles[:, 0], tiles[:, 1])
    given = jnp.where(first_core, tiles[:, 1], tiles[:, 0])
    return kept.reshape(-1, x.shape[1]), given.reshape(-1, x.shape[1])


def sum_rows(kept, given):
    other = lax.ppermute(given.astype(jnp.bfloat16), "core", SWAP)
    both = (kept.astype(jnp.float32) + other.astype(jnp.float32)).astype(jnp.bfloat16)
    tiles = both.reshape(RINGS, both.shape[0] // RINGS, both.shape[1])
    return lax.all_to_all(tiles, "y", 0, 0, tiled=True)


def sum_rows_directly(kept, given):
    other = lax.ppermute(given.astype(jnp.bfloat16), "core", SWAP)
    both = (kept.astype(jnp.float32) + other.astype(jnp.float32)).astype(jnp.bfloat16)
    tiles = both.reshape(RINGS, both.shape[0] // RINGS, both.shape[1])
    y = lax.axis_index("y")
    total = lax.dynamic_index_in_dim(tiles, y, 0, keepdims=False).astype(jnp.float32)
    for pairs in (PAIRS, CROSS, OPPOSITE):
        place = jnp.array([b for _, b in sorted(pairs)], jnp.int32)[y]
        tile = lax.dynamic_index_in_dim(tiles, place, 0, keepdims=False)
        total = total + lax.ppermute(tile, "y", pairs).astype(jnp.float32)
    return total


def total_of(tiles):
    return jnp.sum(tiles.astype(jnp.float32), axis=0)


def sum_ranks(x):
    tiles = lax.all_to_all(x, EXPERT, 0, 0, tiled=True)
    total = jnp.sum(tiles.astype(jnp.float32), axis=0).astype(jnp.bfloat16)
    return lax.all_to_all(jnp.broadcast_to(total[None], x.shape), EXPERT, 0, 0, tiled=True)


def angles_of(places):
    half_width = ROPE // 2
    steps_float = jnp.arange(half_width, dtype=jnp.float32) * (2.0 / ROPE)
    frequency = jnp.exp(-jnp.log(theta_base) * steps_float)
    angles = places.astype(jnp.float32)[:, None] * frequency[None, :]
    return (jnp.cos(angles), jnp.sin(angles))


def rotate(values, cos_table, sin_table):
    half_width = ROPE // 2
    first_half = values[..., :half_width]
    second_half = values[..., half_width:]
    return jnp.concatenate(
        [
            first_half * cos_table - second_half * sin_table,
            second_half * cos_table + first_half * sin_table,
        ],
        axis=-1,
    )


def rotate_back(upstream, cos_table, sin_table):
    half_width = ROPE // 2
    first_half = upstream[..., :half_width]
    second_half = upstream[..., half_width:]
    return jnp.concatenate(
        [
            first_half * cos_table + second_half * sin_table,
            second_half * cos_table - first_half * sin_table,
        ],
        axis=-1,
    )


def matmul(left, right):
    return jnp.dot(left, right, preferred_element_type=jnp.float32)


def matmul_tn(left, right):
    return lax.dot_general(
        left, right, (((0,), (0,)), ((), ())), preferred_element_type=jnp.float32
    )


def matmul_nt(left, right):
    return lax.dot_general(
        left, right, (((1,), (1,)), ((), ())), preferred_element_type=jnp.float32
    )


def norm_forward(values, scales):
    factor = lax.rsqrt(jnp.mean(values * values, axis=-1, keepdims=True) + epsilon)
    return (values * factor * scales, factor)


def norm_backward(values, factor, scales, upstream):
    scaled = upstream * scales
    cubed = factor * factor * factor
    d_values = factor * scaled - values * cubed * jnp.mean(scaled * values, axis=-1, keepdims=True)
    return (d_values, jnp.sum(upstream * values * factor, axis=0))


def split_float(v):
    high = v.astype(jnp.bfloat16)
    low = (v - high.astype(jnp.float32)).astype(jnp.bfloat16)
    return high, low


def to_owners(x):
    return lax.all_to_all(
        x.reshape(RANKS, x.shape[0] // RANKS, x.shape[1]), EXPERT, 0, 0, tiled=True
    ).reshape(x.shape)


HIDDEN = 176
TILE = 256
WIDTH = 512
LOW = 64
LONG = 100_000_000_000
SHORT = 18_000_000_000
VMEM_BYTES = 60 * 1024 * 1024


def dot_nt(left, right):
    return lax.dot_general(
        left, right, (((1,), (1,)), ((), ())), preferred_element_type=jnp.float32
    )


def dot_tn(left, right):
    return lax.dot_general(
        left, right, (((0,), (0,)), ((), ())), preferred_element_type=jnp.float32
    )


def hidden_loop(first, last, carry, step):
    return lax.fori_loop(
        first, last, lambda i, c: step(pl.multiple_of(i * TILE, TILE), TILE, c), carry
    )


def dispatch_kernel(map_ref, rows_ref, tail_ref, out):
    def some(j, carry):
        columns = pl.ds(pl.multiple_of(j * WIDTH, WIDTH), WIDTH)
        out[:, columns] = dot_tn(map_ref[...], rows_ref[:, columns]).astype(jnp.bfloat16)
        return carry

    lax.fori_loop(0, D // WIDTH, some, 0)
    out[:, D:] = dot_tn(map_ref[...], tail_ref[...]).astype(jnp.bfloat16)


def dispatch(slot_map, rows, tail):
    slots, width = slot_map.shape[1], rows.shape[1] + tail.shape[1]
    return pl.pallas_call(
        dispatch_kernel,
        out_shape=jax.ShapeDtypeStruct((slots, width), jnp.bfloat16),
        in_specs=[pl.BlockSpec(memory_space=pltpu.VMEM)] * 3,
        out_specs=pl.BlockSpec(memory_space=pltpu.VMEM),
        compiler_params=pltpu.CompilerParams(vmem_limit_bytes=VMEM_BYTES),
        cost_estimate=pl.CostEstimate(
            flops=2 * slots * slot_map.shape[0] * width, bytes_accessed=8 << 20, transcendentals=0
        ),
        name="dispatch",
    )(slot_map, rows, tail)


def shared_kernel(
    core,
    rows_ref,
    cot_ref,
    w_gate,
    w_up,
    w_down,
    gate_grads,
    up_grads,
    down_grads,
    act,
    kept,
    given,
    sgate,
    sup,
):
    block = rows_ref.shape[0] // (RINGS * CORES)
    gate_value = dot_nt(rows_ref[...], w_gate[...])
    up_value = dot_nt(rows_ref[...], w_up[...])
    back = dot_nt(cot_ref[...], w_down[...])
    sigma = jax.nn.sigmoid(gate_value)
    swish = gate_value * sigma
    act[...] = (swish * up_value).astype(jnp.bfloat16)
    slope = sigma * (1.0 + gate_value * (1.0 - sigma))
    sgate[...] = (back * up_value * slope).astype(jnp.bfloat16)
    sup[...] = (back * swish).astype(jnp.bfloat16)

    def some(j, carry):
        columns = pl.ds(pl.multiple_of(j * WIDTH, WIDTH), WIDTH)
        rows, cot = rows_ref[:, columns], cot_ref[:, columns]
        gate_grads[:, columns] = dot_tn(sgate[...], rows).astype(jnp.bfloat16)
        up_grads[:, columns] = dot_tn(sup[...], rows).astype(jnp.bfloat16)
        down_grads[:, columns] = dot_tn(act[...], cot).astype(jnp.bfloat16)
        value = jnp.dot(sgate[...], w_gate[:, columns], preferred_element_type=jnp.float32)
        value += jnp.dot(sup[...], w_up[:, columns], preferred_element_type=jnp.float32)
        for half in range(CORES):
            for target, chosen in ((kept, core[0] == half), (given, core[0] != half)):

                @pl.when(chosen)
                def _():
                    for chip in range(RINGS):
                        first = (chip * CORES + half) * block
                        target[chip * block : (chip + 1) * block, columns] = value[
                            first : first + block
                        ]

        return carry

    lax.fori_loop(0, D // WIDTH, some, 0)


def shared_experts(core, rows, cot, w_gate, w_up, w_down):
    length, width = rows.shape[0], w_gate.shape[0]
    half = jax.ShapeDtypeStruct((length // 2, D), jnp.float32)
    hidden = (length, width)
    vmem = pl.BlockSpec(memory_space=pltpu.VMEM)
    return pl.pallas_call(
        shared_kernel,
        out_shape=(jax.ShapeDtypeStruct((width, D), jnp.bfloat16),) * 3
        + (jax.ShapeDtypeStruct(hidden, jnp.bfloat16), half, half),
        in_specs=[pl.BlockSpec(memory_space=pltpu.SMEM)] + [vmem] * 5,
        out_specs=(vmem,) * 6,
        scratch_shapes=[pltpu.VMEM(hidden, jnp.bfloat16)] * 2,
        compiler_params=pltpu.CompilerParams(vmem_limit_bytes=VMEM_BYTES),
        cost_estimate=pl.CostEstimate(flops=SHORT, bytes_accessed=20 << 20, transcendentals=0),
        name="shared_experts",
    )(core, rows, cot, w_gate, w_up, w_down)


def expert_outputs_kernel(same, own, taken_hbm, pair, cross, far, *refs):
    outs, taken, sem = refs[:3], refs[3], refs[4]
    copy = pltpu.make_async_copy(taken_hbm.at[pl.ds(0, 3 * HIDDEN)], taken, sem)
    copy.start()
    copy.wait()
    for m, out in enumerate(outs):
        rows = slice(m * HIDDEN, (m + 1) * HIDDEN)
        ours = own[rows, :].astype(jnp.float32) + taken[rows, :].astype(jnp.float32)
        ours += pair[rows, :].astype(jnp.float32)
        others = cross[rows, :].astype(jnp.float32) + far[rows, :].astype(jnp.float32)
        out[same[0]] = ours
        out[1 - same[0]] = others


def expert_outputs(same, own, taken, pair, cross, far):
    vmem = pl.BlockSpec(memory_space=pltpu.VMEM)
    first = pl.BlockSpec(memory_space=pl.ANY)
    return pl.pallas_call(
        expert_outputs_kernel,
        out_shape=(jax.ShapeDtypeStruct((CORES, HIDDEN, D), jnp.float32),) * 3,
        in_specs=[pl.BlockSpec(memory_space=pltpu.SMEM), vmem, first] + [vmem] * 3,
        out_specs=(vmem,) * 3,
        scratch_shapes=[pltpu.VMEM((3 * HIDDEN, D), jnp.bfloat16), pltpu.SemaphoreType.DMA],
        compiler_params=pltpu.CompilerParams(vmem_limit_bytes=VMEM_BYTES),
        cost_estimate=pl.CostEstimate(flops=0, bytes_accessed=20 << 20, transcendentals=0),
        name="expert_outputs",
    )(same, own, taken, pair, cross, far)


def kv_kernel(left, right, out):
    out[...] = jnp.dot(left[...], right[...], preferred_element_type=jnp.float32).astype(
        jnp.bfloat16
    )


def kv_product(left, right):
    vmem = pl.BlockSpec(memory_space=pltpu.VMEM)
    return pl.pallas_call(
        kv_kernel,
        out_shape=jax.ShapeDtypeStruct((left.shape[0], right.shape[1]), jnp.bfloat16),
        in_specs=[vmem] * 2,
        out_specs=vmem,
        compiler_params=pltpu.CompilerParams(vmem_limit_bytes=VMEM_BYTES),
        cost_estimate=pl.CostEstimate(flops=LONG, bytes_accessed=4 << 20, transcendentals=0),
        name="kv_product",
    )(left, right)


def attention_kernel(
    core, query_ref, compressed_ref, x_ref, factor_ref, w_query, w_down, kept, given, gain
):
    block = x_ref.shape[0] // (RINGS * CORES)

    def some(j, carry):
        columns = pl.ds(pl.multiple_of(j * WIDTH, WIDTH), WIDTH)
        scaled = x_ref[:, columns].astype(jnp.float32) * factor_ref[...]
        value = dot_nt(query_ref[...], w_query[columns, :])
        value += jnp.dot(
            compressed_ref[...], w_down[:, columns], preferred_element_type=jnp.float32
        )
        gain[:, columns] = jnp.sum(value * scaled, axis=0, keepdims=True)
        value = value.astype(jnp.bfloat16)
        for half in range(CORES):
            for target, chosen in ((kept, core[0] == half), (given, core[0] != half)):

                @pl.when(chosen)
                def _():
                    for chip in range(RINGS):
                        first = (chip * CORES + half) * block
                        target[chip * block : (chip + 1) * block, columns] = value[
                            first : first + block
                        ]

        return carry

    lax.fori_loop(0, D // WIDTH, some, 0)


def attention_rows(core, query, compressed, x, factor, w_query, w_down):
    half = jax.ShapeDtypeStruct((x.shape[0] // 2, D), jnp.bfloat16)
    vmem = pl.BlockSpec(memory_space=pltpu.VMEM)
    return pl.pallas_call(
        attention_kernel,
        out_shape=(half, half, jax.ShapeDtypeStruct((1, D), jnp.float32)),
        in_specs=[pl.BlockSpec(memory_space=pltpu.SMEM)] + [vmem] * 6,
        out_specs=(vmem,) * 3,
        compiler_params=pltpu.CompilerParams(vmem_limit_bytes=VMEM_BYTES),
        cost_estimate=pl.CostEstimate(flops=LONG, bytes_accessed=10 << 20, transcendentals=0),
        name="attention_rows",
    )(core, query, compressed, x, factor, w_query, w_down)


def expert_kernel(*refs):
    expert, x_hbm, y_hbm = refs[:3]
    blocks = refs[3:11]
    back, gate_out, up_out, act_out = refs[11:15]
    x_ref, y_ref, w_gate, w_up, w_down, sems = refs[15:]
    total = w_gate.shape[0]
    copies = [
        pltpu.make_async_copy(x_hbm, x_ref, sems.at[0]),
        pltpu.make_async_copy(y_hbm, y_ref, sems.at[1]),
    ]
    for i, block in enumerate(blocks):
        rows = pl.ds(i * HIDDEN, HIDDEN)
        for m, w in enumerate((w_gate, w_up, w_down)):
            copies.append(
                pltpu.make_async_copy(
                    block.at[pl.ds(m * HIDDEN, HIDDEN)], w.at[rows], sems.at[2 + 3 * i + m]
                )
            )
    for copy in copies:
        copy.start()
    half = 2 + len(copies[2:]) // 2
    for copy in copies[:half]:
        copy.wait()
    lanes = lax.broadcasted_iota(jnp.int32, (x_ref.shape[0], 128), 1)
    high_lane, low_lane = lanes == expert[0], lanes == expert[0] + LOW
    tail = x_ref[:, D:].astype(jnp.float32)
    gate = jnp.sum(jnp.where(high_lane | low_lane, tail, 0.0), axis=-1, keepdims=True)

    def hidden(start, width, summed):
        rows = pl.ds(start, width)
        x = x_ref[:, :D]
        gate_value = dot_nt(x, w_gate[rows, :])
        up_value = dot_nt(x, w_up[rows, :])
        raw = dot_nt(y_ref[...], w_down[rows, :])
        sigma = jax.nn.sigmoid(gate_value)
        swish = gate_value * sigma
        act = swish * up_value
        summed = summed + jnp.sum(raw * act, axis=-1, keepdims=True)
        raw = raw * gate
        slope = sigma * (1.0 + gate_value * (1.0 - sigma))
        gate_out[:, rows] = (raw * up_value * slope).astype(jnp.bfloat16)
        up_out[:, rows] = (raw * swish).astype(jnp.bfloat16)
        act_out[:, rows] = (act * gate).astype(jnp.bfloat16)
        return summed

    ready = (total // 2) // TILE
    whole = total // TILE
    summed = hidden_loop(0, ready, jnp.zeros((x_ref.shape[0], 1), jnp.float32), hidden)
    for copy in copies[half:]:
        copy.wait()
    summed = hidden_loop(ready, whole, summed, hidden)
    if total % TILE:
        summed = hidden(whole * TILE, total % TILE, summed)
    high = summed.astype(jnp.bfloat16).astype(jnp.float32)
    back[:, D:] = jnp.where(
        high_lane, high, jnp.where(low_lane, summed - high, 0.0)
    ).astype(jnp.bfloat16)

    def inward(j, carry):
        columns = pl.ds(pl.multiple_of(j * WIDTH, WIDTH), WIDTH)
        value = jnp.dot(gate_out[...], w_gate[:, columns], preferred_element_type=jnp.float32)
        value += jnp.dot(up_out[...], w_up[:, columns], preferred_element_type=jnp.float32)
        back[:, columns] = value.astype(jnp.bfloat16)
        return carry

    lax.fori_loop(0, D // WIDTH, inward, 0)


def expert_rows(expert, x, g_y, blocks):
    slots = x.shape[0]
    total = HIDDEN * len(blocks)
    bf16 = jnp.bfloat16
    anywhere = pl.BlockSpec(memory_space=pl.ANY)
    vmem = pl.BlockSpec(memory_space=pltpu.VMEM)
    return pl.pallas_call(
        expert_kernel,
        out_shape=(jax.ShapeDtypeStruct(x.shape, bf16),)
        + (jax.ShapeDtypeStruct((slots, total), bf16),) * 3,
        in_specs=[pl.BlockSpec(memory_space=pltpu.SMEM)] + [anywhere] * (2 + len(blocks)),
        out_specs=(vmem,) * 4,
        scratch_shapes=[
            pltpu.VMEM(x.shape, bf16),
            pltpu.VMEM((slots, D), bf16),
            pltpu.VMEM((total, D), bf16),
            pltpu.VMEM((total, D), bf16),
            pltpu.VMEM((total, D), bf16),
            pltpu.SemaphoreType.DMA((2 + 3 * len(blocks),)),
        ],
        compiler_params=pltpu.CompilerParams(vmem_limit_bytes=VMEM_BYTES),
        cost_estimate=pl.CostEstimate(
            flops=10 * slots * total * D, bytes_accessed=28 << 20, transcendentals=slots * total
        ),
        name="expert_rows",
    )(expert, x, g_y, *blocks)


def expert_weights_kernel(*refs):
    x_ref, y_ref, gate_ref, up_ref, act_ref = refs[:5]
    blocks = refs[5:13]
    out, places = refs[13], refs[14:19]
    w_down, holds, sems = refs[19], refs[20:23], refs[23]
    total = gate_ref.shape[1]
    loads = []
    for i, block in enumerate(blocks):
        loads.append(
            pltpu.make_async_copy(
                block.at[pl.ds(2 * HIDDEN, HIDDEN)],
                w_down.at[pl.ds(i * HIDDEN, HIDDEN)],
                sems.at[i],
            )
        )
        loads[-1].start()
    copies = []
    for m, (left, right) in enumerate(((gate_ref, x_ref), (up_ref, x_ref), (act_ref, y_ref))):

        def hidden(start, width, carry):
            rows = pl.ds(start, width)
            holds[m][rows, :] = dot_tn(left[:, rows], right[:, :D]).astype(jnp.bfloat16)
            return carry

        hidden_loop(0, total // TILE, 0, hidden)
        if total % TILE:
            hidden(total // TILE * TILE, total % TILE, 0)
        for i in range(len(blocks)):
            first = m + 3 * max(i - RINGS, 0)
            place = places[min(i, RINGS)].at[pl.ds(first * HIDDEN, HIDDEN)]
            source = holds[m].at[pl.ds(i * HIDDEN, HIDDEN)]
            copies.append(
                pltpu.make_async_copy(source, place, sems.at[len(blocks) * (m + 1) + i])
            )
            copies[-1].start()
    for load in loads:
        load.wait()

    def outward(j, carry):
        columns = pl.ds(pl.multiple_of(j * WIDTH, WIDTH), WIDTH)
        value = jnp.dot(act_ref[...], w_down[:, columns], preferred_element_type=jnp.float32)
        out[:, columns] = value.astype(jnp.bfloat16)
        return carry

    lax.fori_loop(0, D // WIDTH, outward, 0)
    for copy in copies:
        copy.wait()


def expert_weights(x, g_y, gate, up, act, blocks):
    slots, total = gate.shape
    bf16 = jnp.bfloat16
    anywhere = pl.BlockSpec(memory_space=pl.ANY)
    vmem = pl.BlockSpec(memory_space=pltpu.VMEM)
    sizes = (3 * HIDDEN,) * RINGS + (3 * HIDDEN * RINGS,)
    return pl.pallas_call(
        expert_weights_kernel,
        out_shape=(jax.ShapeDtypeStruct((slots, D), bf16),)
        + tuple(jax.ShapeDtypeStruct((size, D), bf16) for size in sizes),
        in_specs=[vmem] * 5 + [anywhere] * len(blocks),
        out_specs=(vmem,) + (anywhere,) * 5,
        scratch_shapes=[pltpu.VMEM((total, D), bf16)] * 4
        + [pltpu.SemaphoreType.DMA((4 * len(blocks),))],
        compiler_params=pltpu.CompilerParams(vmem_limit_bytes=VMEM_BYTES),
        cost_estimate=pl.CostEstimate(
            flops=LONG, bytes_accessed=34 << 20, transcendentals=0
        ),
        name="expert_weights",
    )(x, g_y, gate, up, act, *blocks)


def shards(
    layer_input,
    attn_gain,
    w_query,
    w_kv_down,
    kv_gain,
    w_kv_up,
    w_out,
    ffn_gain,
    w_router,
    routes,
    expert_gate,
    expert_up_projection,
    expert_down,
    shared_gate,
    shared_up,
    shared_down,
    cotangent,
):
    length = layer_input.shape[0]
    rows = length // (RINGS * CORES)
    y, core = lax.axis_index("y"), lax.axis_index("core")
    qk_width = NOPE + ROPE
    heads_here = w_query.shape[1] // qk_width
    score_scale = qk_width ** (-0.5)
    experts_total = w_router.shape[1]
    first_core = core == 0
    second_expert = y >= RINGS // 2

    def block_of(expert):
        parts = (
            jnp.swapaxes(expert_gate, 1, 2),
            jnp.swapaxes(expert_up_projection, 1, 2),
            expert_down,
        )
        return jnp.concatenate(
            [lax.dynamic_index_in_dim(part, expert, 0, keepdims=False) for part in parts], axis=0
        )

    same = second_expert.astype(jnp.int32)
    same_block, other_block = block_of(same), block_of(1 - same)
    weights = [
        same_block,
        lax.ppermute(same_block, "y", PAIRS),
        lax.ppermute(other_block, "y", CROSS),
    ]

    places = jnp.arange(length, dtype=jnp.int32)
    own_start = (y * CORES + core) * rows
    cot_all = gather_rows(cotangent)
    cot_rows = cotangent.astype(jnp.float32)

    def own(table):
        return lax.dynamic_slice_in_dim(table, own_start, rows, 0)

    def parts_of(table):
        return by_core(table, first_core)

    expert_ids = jnp.arange(experts_total, dtype=jnp.int32)
    picked = jnp.zeros((length, experts_total), jnp.float32)
    for route in range(TOP):
        picked = picked + (routes[:, route : route + 1] == expert_ids[None, :]).astype(jnp.float32)
    earlier = (places[:, None] > places[None, :]).astype(jnp.bfloat16)
    before = matmul(earlier, picked.astype(jnp.bfloat16))
    share = 128 // RINGS
    quarter = (y % 2) * CORES + core
    slots = jnp.arange(RANKS * share, dtype=jnp.int32)
    expert_of_slot = (experts_total // RANKS) * (slots // share) + same
    spread = (expert_ids[:, None] == expert_of_slot[None, :]).astype(jnp.bfloat16)
    place_of = matmul((picked * (before + 1.0)).astype(jnp.bfloat16), spread)
    slot_number = (slots % share + share * quarter + 1).astype(jnp.float32)
    slot_map = (place_of == slot_number[None, :]).astype(jnp.bfloat16)
    slot_parts = parts_of(slot_map)
    g_y_sent = matmul_tn(slot_map, cot_all).astype(jnp.bfloat16)
    g_y = to_owners(g_y_sent)

    cos_table, sin_table = angles_of(places)
    input_full = layer_input.astype(jnp.float32)
    normed_full, factor_one = norm_forward(input_full, attn_gain)
    normed_a = normed_full.astype(jnp.bfloat16)
    query_raw = matmul(normed_a, w_query).reshape(length, heads_here, qk_width)
    query_turned = rotate(query_raw[..., NOPE:], cos_table[:, None, :], sin_table[:, None, :])
    query = jnp.concatenate([query_raw[..., :NOPE], query_turned], axis=-1).astype(jnp.bfloat16)
    compressed = matmul(normed_a, w_kv_down)
    latent_raw = compressed[:, :KV_RANK]
    latent_normed, factor_kv = norm_forward(latent_raw, kv_gain)
    latent = latent_normed.astype(jnp.bfloat16)
    key_rope = rotate(compressed[:, KV_RANK:], cos_table, sin_table).astype(jnp.bfloat16)
    key_value = (
        matmul(latent, w_kv_up).astype(jnp.bfloat16).reshape(length, heads_here, NOPE + VDIM)
    )
    key_nope = key_value[..., :NOPE]
    values_all = key_value[..., NOPE:]
    causal = places[:, None] >= places[None, :]

    def scores_of(query):
        scores = jnp.einsum(
            "qhd,khd->hqk", query[..., :NOPE], key_nope, preferred_element_type=jnp.float32
        )
        scores = scores + jnp.einsum(
            "qhd,kd->hqk", query[..., NOPE:], key_rope, preferred_element_type=jnp.float32
        )
        return jnp.where(causal[None], scores * score_scale, -1e30)

    scores = scores_of(query)
    top_score = jnp.max(scores, axis=-1, keepdims=True)
    powered = jnp.exp(scores - top_score)
    total = jnp.sum(powered, axis=-1, keepdims=True)
    probs = (powered / total).astype(jnp.bfloat16)
    log_totals = top_score + jnp.log(total)
    heads_out = (
        jnp.einsum("hqk,khd->qhd", probs, values_all, preferred_element_type=jnp.float32)
        .astype(jnp.bfloat16)
        .reshape(length, heads_here * VDIM)
    )
    attn_kept, attn_given = parts_of(matmul(heads_out, w_out).astype(jnp.bfloat16))
    attended = sum_rows_directly(after(attn_kept, g_y_sent, *weights[1:]), attn_given)
    residual = own(input_full) + attended
    normed_two, factor_two = norm_forward(residual, ffn_gain)
    normed_rows = normed_two.astype(jnp.bfloat16)
    normed_f = gather_rows(normed_rows)
    weights.append(lax.ppermute(after(other_block, normed_f), "y", OPPOSITE))

    sigmoid_all = jax.nn.sigmoid(matmul(normed_f, w_router))
    selected = sigmoid_all * picked
    sel_total = jnp.sum(selected, axis=-1, keepdims=True)
    gates = route_scale * selected / sel_total
    high, low = split_float(gates)
    gap = jnp.zeros((length, LOW - experts_total), jnp.bfloat16)
    sent = dispatch(slot_map, normed_f, jnp.concatenate([high, gap, low, gap], axis=1))
    arrived = to_owners(after(sent, g_y))

    core_index = core.reshape(1).astype(jnp.int32)
    *grads_shared, shared_act, kept_back, given_back = shared_experts(
        core_index,
        after(normed_f, sent),
        cot_all,
        jnp.swapaxes(shared_gate, 0, 1),
        jnp.swapaxes(shared_up, 0, 1),
        shared_down,
    )

    shared_back = (kept_back, given_back)

    arrived = after(arrived, *shared_back)
    last = after(weights[-1], arrived)
    weights = weights + [lax.ppermute(w, "core", SWAP) for w in (*weights[:-1], last)]
    expert_here = 2 * lax.axis_index("x") * 4 + 2 * lax.axis_index("z") + same
    back, g_gate, g_up, act = expert_rows(
        expert_here.reshape(1).astype(jnp.int32), arrived, g_y, weights
    )
    out, *block_grads = expert_weights(
        arrived, g_y, g_gate, g_up, act, weights
    )
    back = after(to_owners(back), *block_grads)

    taken_grads = lax.ppermute(block_grads[RINGS], "core", SWAP)
    grads_sent = [
        (
            block_grads[r].astype(jnp.float32)
            + taken_grads[3 * HIDDEN * r : 3 * HIDDEN * (r + 1)].astype(jnp.float32)
        ).astype(jnp.bfloat16)
        for r in range(1, RINGS)
    ]

    summed = sum_rows_directly(
        *(
            matmul(a, back) + jnp.pad(b, ((0, 0), (0, 128)))
            for a, b in zip(slot_parts, shared_back)
        )
    )
    g_gate_rows = summed[:, D : D + experts_total] + summed[:, D + LOW : D + LOW + experts_total]

    sigma_rows, picked_rows, total_rows = own(sigmoid_all), own(picked), own(sel_total)
    sel_rows = sigma_rows * picked_rows
    grad_sel = route_scale * (
        g_gate_rows / total_rows
        - jnp.sum(g_gate_rows * sel_rows, axis=-1, keepdims=True) / (total_rows * total_rows)
    )
    grad_logits = (grad_sel * picked_rows * sigma_rows * (1.0 - sigma_rows)).astype(jnp.bfloat16)
    grad_w_router = matmul_tn(grad_logits, normed_rows)
    grad_normed = summed[:, :D] + matmul_nt(grad_logits, w_router)
    grad_from_norm, grad_ffn_gain = norm_backward(residual, factor_two, ffn_gain, grad_normed)
    grad_residual = cot_rows + grad_from_norm
    grad_residual_low = grad_residual.astype(jnp.bfloat16)
    grad_attended = gather_rows(grad_residual_low)
    returned = to_owners(after(out, grad_residual_low))

    grad_w_out = matmul_tn(heads_out, grad_attended).astype(jnp.bfloat16)

    grad_heads = (
        matmul_nt(grad_attended, w_out).astype(jnp.bfloat16).reshape(length, heads_here, VDIM)
    )
    probs_full = jnp.exp(scores_of(query) - log_totals)
    grad_probs = jnp.einsum(
        "qhd,khd->hqk", grad_heads, values_all, preferred_element_type=jnp.float32
    )
    grad_scores = (
        probs_full * (grad_probs - jnp.sum(grad_probs * probs_full, axis=-1, keepdims=True))
    ).astype(jnp.bfloat16)
    grad_query_nope = (
        jnp.einsum("hqk,khd->qhd", grad_scores, key_nope, preferred_element_type=jnp.float32)
        * score_scale
    )
    grad_query_rope = (
        jnp.einsum("hqk,kd->qhd", grad_scores, key_rope, preferred_element_type=jnp.float32)
        * score_scale
    )
    grad_key_nope = (
        jnp.einsum(
            "hqk,qhd->khd", grad_scores, query[..., :NOPE], preferred_element_type=jnp.float32
        )
        * score_scale
    )
    grad_key_rope = (
        jnp.einsum(
            "hqk,qhd->kd", grad_scores, query[..., NOPE:], preferred_element_type=jnp.float32
        )
        * score_scale
    )
    grad_values = jnp.einsum(
        "hqk,qhd->khd",
        probs_full.astype(jnp.bfloat16),
        grad_heads,
        preferred_element_type=jnp.float32,
    )
    grad_query_back = rotate_back(
        grad_query_rope, cos_table[:, None, :], sin_table[:, None, :]
    )
    grad_query = (
        jnp.concatenate([grad_query_nope, grad_query_back], axis=-1)
        .astype(jnp.bfloat16)
        .reshape(length, heads_here * qk_width)
    )
    grad_w_query = matmul_tn(normed_a, grad_query).astype(jnp.bfloat16)
    grad_key_value = (
        jnp.concatenate([grad_key_nope, grad_values], axis=-1)
        .astype(jnp.bfloat16)
        .reshape(length, heads_here * (NOPE + VDIM))
    )
    grad_w_kv_up = matmul_tn(latent, grad_key_value).astype(jnp.bfloat16)
    grad_latent_normed = matmul_nt(grad_key_value, w_kv_up)
    grad_latent, grad_kv_gain = norm_backward(latent_raw, factor_kv, kv_gain, grad_latent_normed)
    grad_rope_part = rotate_back(grad_key_rope, cos_table, sin_table)
    grad_compressed = jnp.concatenate([grad_latent, grad_rope_part], axis=-1).astype(jnp.bfloat16)
    local_grads = (grad_w_out, grad_w_query, grad_w_kv_up, *grads_shared)
    grad_w_out, grad_w_query, grad_w_kv_up, *grads_shared = lax.psum(local_grads, EXPERT)
    kept, given, grad_attn_gain = attention_rows(
        core_index,
        grad_query,
        grad_compressed,
        layer_input,
        factor_one,
        w_query,
        jnp.swapaxes(w_kv_down, 0, 1),
    )

    parts = RINGS * CORES
    kv_share = grad_compressed.shape[1] // parts
    columns = D // parts
    gains = jnp.concatenate(
        [
            grad_attn_gain.reshape(parts, columns),
            grad_ffn_gain.reshape(parts, columns),
            grad_kv_gain.reshape(parts, KV_RANK // parts),
        ],
        axis=1,
    )
    gains = jnp.pad(gains, ((0, 0), (0, 16 * length // 2 - gains.shape[1])))
    bundle = jnp.concatenate(
        [
            jnp.swapaxes(grad_compressed, 0, 1).reshape(parts, kv_share, length),
            jnp.swapaxes(grad_w_router.reshape(experts_total, parts, columns), 0, 1)
            .reshape(parts, experts_total * columns // length, length)
            .astype(jnp.bfloat16),
            gains.reshape(parts, 8, length).astype(jnp.bfloat16),
        ],
        axis=1,
    )
    bundle = after(bundle, returned, *local_grads)

    def last_sums():
        tiles = lax.all_to_all(bundle, GROUP, 0, 0, tiled=True)
        slices = total_of(tiles).astype(jnp.bfloat16)
        pair_grads = lax.ppermute(grads_sent[0], "y", PAIRS)
        cross_grads = lax.ppermute(grads_sent[1], "y", CROSS)
        act_parts = parts_of(shared_act)
        both_sums = sum_rows_directly(
            *(
                jnp.concatenate(
                    [c, (matmul(a, returned) + matmul(b, shared_down)).astype(jnp.bfloat16)], axis=1
                )
                for a, b, c in zip(slot_parts, act_parts, (kept, given))
            )
        )
        grad_normed_one, routed_and_shared = both_sums[:, :D], both_sums[:, D:]
        output = (residual + routed_and_shared).astype(jnp.bfloat16)
        grad_from_first, _ = norm_backward(
            own(input_full), own(factor_one), attn_gain, grad_normed_one
        )
        grad_input = grad_residual + grad_from_first
        far_grads = lax.ppermute(
            after(grads_sent[2], slices), "y", OPPOSITE
        )
        kv_slice = kv_product(slices[:kv_share], normed_a)
        other_rows = slices[kv_share:].reshape(-1, D)
        rest = jnp.zeros((80 - kv_share - other_rows.shape[0], D), jnp.bfloat16)
        replicated = jnp.concatenate([kv_slice, other_rows, rest], axis=0)
        replicated = jnp.swapaxes(replicated.reshape(80, RANKS, D // RANKS), 0, 1)
        replicated = sum_ranks(replicated)
        expert_grads = expert_outputs(
            same.reshape(1), block_grads[0], taken_grads, pair_grads, cross_grads, far_grads
        )
        replicated = after(
            replicated, pair_grads
        )
        replicated = gather_rows_directly(
            replicated.reshape(RANKS * 80, D // RANKS), first_core, expert_grads
        )
        return grad_input, replicated, output, expert_grads

    grad_input, replicated, output, expert_grads = as_unit(
        last_sums, routes[0, 0] >= 0
    )
    replicated = replicated.reshape(parts, RANKS, 80, D // RANKS)

    def unpacked(first, last):
        piece = jnp.swapaxes(replicated[:, :, first:last], 1, 2)
        return piece.reshape(parts, last - first, D).astype(jnp.float32)

    grad_w_kv_down = jnp.swapaxes(unpacked(0, kv_share).reshape(-1, D), 0, 1)
    router_rows = experts_total * columns // D
    grad_w_router = (
        jnp.swapaxes(
            unpacked(kv_share, kv_share + router_rows).reshape(parts, experts_total, columns), 0, 1
        )
        .reshape(experts_total, D)
        .T
    )
    gains = unpacked(kv_share + router_rows, kv_share + router_rows + 1)[:, 0]
    grad_attn_gain = gains[:, :columns].reshape(D)
    grad_ffn_gain = gains[:, columns : 2 * columns].reshape(D)
    grad_kv_gain = gains[:, 2 * columns : 2 * columns + KV_RANK // parts].reshape(KV_RANK)
    grads_shared = [grad.astype(jnp.float32) for grad in grads_shared]
    return (
        output,
        grad_input,
        grad_attn_gain,
        grad_w_query.astype(jnp.float32),
        grad_w_kv_down,
        grad_kv_gain,
        grad_w_kv_up.astype(jnp.float32),
        grad_w_out.astype(jnp.float32),
        grad_ffn_gain,
        grad_w_router,
        jnp.swapaxes(expert_grads[0], 1, 2),
        jnp.swapaxes(expert_grads[1], 1, 2),
        expert_grads[2],
        grads_shared[0].T,
        grads_shared[1].T,
        grads_shared[2],
    )


def solution(mesh):
    split = Mesh(mesh.devices.reshape(4, 4, RINGS, CORES), ("x", "z", "y", "core"))
    return jax.shard_map(
        shards,
        mesh=split,
        in_specs=(
            P(EXPERT, None),
            P(),
            P(None, GROUP),
            P(),
            P(),
            P(None, GROUP),
            P(GROUP, None),
            P(),
            P(),
            P(EXPERT, None),
            P(EXPERT, None, GROUP),
            P(EXPERT, None, GROUP),
            P(EXPERT, GROUP, None),
            P(None, GROUP),
            P(None, GROUP),
            P(GROUP, None),
            P(("x", "z", "y", "core"), None),
        ),
        out_specs=(
            P(("x", "z", "y", "core"), None),
            P(("x", "z", "y", "core"), None),
            P(),
            P(None, GROUP),
            P(),
            P(),
            P(None, GROUP),
            P(GROUP, None),
            P(),
            P(),
            P(EXPERT, None, GROUP),
            P(EXPERT, None, GROUP),
            P(EXPERT, GROUP, None),
            P(None, GROUP),
            P(None, GROUP),
            P(GROUP, None),
        ),
        check_vma=False,
    )
```

```python
import jax
import jax.numpy as jnp
from jax import lax
from jax.experimental import pallas as pl
from jax.experimental.pallas import tpu as pltpu
from jax.sharding import Mesh, PartitionSpec as P

D = 2048
NOPE = 128
ROPE = 64
VDIM = 128
KV_RANK = 512
TOP = 6
RANKS = 16
RINGS = 4
CORES = 2

epsilon = 1e-06
route_scale = 2.446
theta_base = 50000.0

EXPERT = ("x", "z")
GROUP = ("y", "core")
SWAP = [(0, 1), (1, 0)]
PAIRS = [(0, 1), (1, 0), (2, 3), (3, 2)]
OPPOSITE = [(0, 2), (2, 0), (1, 3), (3, 1)]
CROSS = [(1, 2), (2, 1), (3, 0), (0, 3)]


def after(x, *finished):
    return lax.optimization_barrier((x, *finished))[0]


def gather_rows(x):
    return lax.all_gather(x, GROUP, axis=0, tiled=True)


def gather_rows_directly(x, first_core, beside):
    copies = jnp.broadcast_to(x[None], (RINGS, *x.shape))
    mine = lax.all_to_all(copies, "y", 0, 0, tiled=True)
    mine = after(mine, *beside)
    other = lax.ppermute(mine, "core", SWAP)
    first, second = jnp.where(first_core, mine, other), jnp.where(first_core, other, mine)
    return jnp.stack([first, second], axis=1).reshape(-1, x.shape[1])


def as_unit(work, always):
    shapes = jax.eval_shape(work)
    return lax.cond(
        always, work, lambda: jax.tree.map(lambda a: jnp.zeros(a.shape, a.dtype), shapes)
    )


def by_core(x, first_core):
    tiles = x.reshape(RINGS, CORES, x.shape[0] // (RINGS * CORES), x.shape[1])
    kept = jnp.where(first_core, tiles[:, 0], tiles[:, 1])
    given = jnp.where(first_core, tiles[:, 1], tiles[:, 0])
    return kept.reshape(-1, x.shape[1]), given.reshape(-1, x.shape[1])


def sum_rows(kept, given):
    other = lax.ppermute(given.astype(jnp.bfloat16), "core", SWAP)
    both = (kept.astype(jnp.float32) + other.astype(jnp.float32)).astype(jnp.bfloat16)
    tiles = both.reshape(RINGS, both.shape[0] // RINGS, both.shape[1])
    return lax.all_to_all(tiles, "y", 0, 0, tiled=True)


def sum_rows_directly(kept, given):
    other = lax.ppermute(given.astype(jnp.bfloat16), "core", SWAP)
    both = (kept.astype(jnp.float32) + other.astype(jnp.float32)).astype(jnp.bfloat16)
    tiles = both.reshape(RINGS, both.shape[0] // RINGS, both.shape[1])
    y = lax.axis_index("y")
    total = lax.dynamic_index_in_dim(tiles, y, 0, keepdims=False).astype(jnp.float32)
    for pairs in (PAIRS, CROSS, OPPOSITE):
        place = jnp.array([b for _, b in sorted(pairs)], jnp.int32)[y]
        tile = lax.dynamic_index_in_dim(tiles, place, 0, keepdims=False)
        total = total + lax.ppermute(tile, "y", pairs).astype(jnp.float32)
    return total


def total_of(tiles):
    return jnp.sum(tiles.astype(jnp.float32), axis=0)


def sum_ranks(x):
    tiles = lax.all_to_all(x, EXPERT, 0, 0, tiled=True)
    total = jnp.sum(tiles.astype(jnp.float32), axis=0).astype(jnp.bfloat16)
    return lax.all_to_all(jnp.broadcast_to(total[None], x.shape), EXPERT, 0, 0, tiled=True)


def angles_of(places):
    half_width = ROPE // 2
    steps_float = jnp.arange(half_width, dtype=jnp.float32) * (2.0 / ROPE)
    frequency = jnp.exp(-jnp.log(theta_base) * steps_float)
    angles = places.astype(jnp.float32)[:, None] * frequency[None, :]
    return (jnp.cos(angles), jnp.sin(angles))


def rotate(values, cos_table, sin_table):
    half_width = ROPE // 2
    first_half = values[..., :half_width]
    second_half = values[..., half_width:]
    return jnp.concatenate(
        [
            first_half * cos_table - second_half * sin_table,
            second_half * cos_table + first_half * sin_table,
        ],
        axis=-1,
    )


def rotate_back(upstream, cos_table, sin_table):
    half_width = ROPE // 2
    first_half = upstream[..., :half_width]
    second_half = upstream[..., half_width:]
    return jnp.concatenate(
        [
            first_half * cos_table + second_half * sin_table,
            second_half * cos_table - first_half * sin_table,
        ],
        axis=-1,
    )


def matmul(left, right):
    return jnp.dot(left, right, preferred_element_type=jnp.float32)


def matmul_tn(left, right):
    return lax.dot_general(
        left, right, (((0,), (0,)), ((), ())), preferred_element_type=jnp.float32
    )


def matmul_nt(left, right):
    return lax.dot_general(
        left, right, (((1,), (1,)), ((), ())), preferred_element_type=jnp.float32
    )


def norm_forward(values, scales):
    factor = lax.rsqrt(jnp.mean(values * values, axis=-1, keepdims=True) + epsilon)
    return (values * factor * scales, factor)


def norm_backward(values, factor, scales, upstream):
    scaled = upstream * scales
    cubed = factor * factor * factor
    d_values = factor * scaled - values * cubed * jnp.mean(scaled * values, axis=-1, keepdims=True)
    return (d_values, jnp.sum(upstream * values * factor, axis=0))


def split_float(v):
    high = v.astype(jnp.bfloat16)
    low = (v - high.astype(jnp.float32)).astype(jnp.bfloat16)
    return high, low


def to_owners(x):
    return lax.all_to_all(
        x.reshape(RANKS, x.shape[0] // RANKS, x.shape[1]), EXPERT, 0, 0, tiled=True
    ).reshape(x.shape)


HIDDEN = 176
TILE = 256
WIDTH = 512
LOW = 64
LONG = 100_000_000_000
SHORT = 18_000_000_000
VMEM_BYTES = 60 * 1024 * 1024


def dot_nt(left, right):
    return lax.dot_general(
        left, right, (((1,), (1,)), ((), ())), preferred_element_type=jnp.float32
    )


def dot_tn(left, right):
    return lax.dot_general(
        left, right, (((0,), (0,)), ((), ())), preferred_element_type=jnp.float32
    )


def hidden_loop(first, last, carry, step):
    return lax.fori_loop(
        first, last, lambda i, c: step(pl.multiple_of(i * TILE, TILE), TILE, c), carry
    )


def dispatch_kernel(map_ref, rows_ref, tail_ref, out):
    def some(j, carry):
        columns = pl.ds(pl.multiple_of(j * WIDTH, WIDTH), WIDTH)
        out[:, columns] = dot_tn(map_ref[...], rows_ref[:, columns]).astype(jnp.bfloat16)
        return carry

    lax.fori_loop(0, D // WIDTH, some, 0)
    out[:, D:] = dot_tn(map_ref[...], tail_ref[...]).astype(jnp.bfloat16)


def dispatch(slot_map, rows, tail):
    slots, width = slot_map.shape[1], rows.shape[1] + tail.shape[1]
    return pl.pallas_call(
        dispatch_kernel,
        out_shape=jax.ShapeDtypeStruct((slots, width), jnp.bfloat16),
        in_specs=[pl.BlockSpec(memory_space=pltpu.VMEM)] * 3,
        out_specs=pl.BlockSpec(memory_space=pltpu.VMEM),
        compiler_params=pltpu.CompilerParams(vmem_limit_bytes=VMEM_BYTES),
        cost_estimate=pl.CostEstimate(
            flops=2 * slots * slot_map.shape[0] * width, bytes_accessed=8 << 20, transcendentals=0
        ),
        name="dispatch",
    )(slot_map, rows, tail)


def shared_kernel(
    core,
    rows_ref,
    cot_ref,
    w_gate,
    w_up,
    w_down,
    gate_grads,
    up_grads,
    down_grads,
    act,
    kept,
    given,
    sgate,
    sup,
):
    block = rows_ref.shape[0] // (RINGS * CORES)
    gate_value = dot_nt(rows_ref[...], w_gate[...])
    up_value = dot_nt(rows_ref[...], w_up[...])
    back = dot_nt(cot_ref[...], w_down[...])
    sigma = jax.nn.sigmoid(gate_value)
    swish = gate_value * sigma
    act[...] = (swish * up_value).astype(jnp.bfloat16)
    slope = sigma * (1.0 + gate_value * (1.0 - sigma))
    sgate[...] = (back * up_value * slope).astype(jnp.bfloat16)
    sup[...] = (back * swish).astype(jnp.bfloat16)

    def some(j, carry):
        columns = pl.ds(pl.multiple_of(j * WIDTH, WIDTH), WIDTH)
        rows, cot = rows_ref[:, columns], cot_ref[:, columns]
        gate_grads[:, columns] = dot_tn(sgate[...], rows).astype(jnp.bfloat16)
        up_grads[:, columns] = dot_tn(sup[...], rows).astype(jnp.bfloat16)
        down_grads[:, columns] = dot_tn(act[...], cot).astype(jnp.bfloat16)
        value = jnp.dot(sgate[...], w_gate[:, columns], preferred_element_type=jnp.float32)
        value += jnp.dot(sup[...], w_up[:, columns], preferred_element_type=jnp.float32)
        for half in range(CORES):
            for target, chosen in ((kept, core[0] == half), (given, core[0] != half)):

                @pl.when(chosen)
                def _():
                    for chip in range(RINGS):
                        first = (chip * CORES + half) * block
                        target[chip * block : (chip + 1) * block, columns] = value[
                            first : first + block
                        ]

        return carry

    lax.fori_loop(0, D // WIDTH, some, 0)


def shared_experts(core, rows, cot, w_gate, w_up, w_down):
    length, width = rows.shape[0], w_gate.shape[0]
    half = jax.ShapeDtypeStruct((length // 2, D), jnp.float32)
    hidden = (length, width)
    vmem = pl.BlockSpec(memory_space=pltpu.VMEM)
    return pl.pallas_call(
        shared_kernel,
        out_shape=(jax.ShapeDtypeStruct((width, D), jnp.bfloat16),) * 3
        + (jax.ShapeDtypeStruct(hidden, jnp.bfloat16), half, half),
        in_specs=[pl.BlockSpec(memory_space=pltpu.SMEM)] + [vmem] * 5,
        out_specs=(vmem,) * 6,
        scratch_shapes=[pltpu.VMEM(hidden, jnp.bfloat16)] * 2,
        compiler_params=pltpu.CompilerParams(vmem_limit_bytes=VMEM_BYTES),
        cost_estimate=pl.CostEstimate(flops=SHORT, bytes_accessed=20 << 20, transcendentals=0),
        name="shared_experts",
    )(core, rows, cot, w_gate, w_up, w_down)


def expert_outputs_kernel(same, own, taken_hbm, pair, cross, far, *refs):
    outs, taken, sem = refs[:3], refs[3], refs[4]
    copy = pltpu.make_async_copy(taken_hbm.at[pl.ds(0, 3 * HIDDEN)], taken, sem)
    copy.start()
    copy.wait()
    for m, out in enumerate(outs):
        rows = slice(m * HIDDEN, (m + 1) * HIDDEN)
        ours = own[rows, :].astype(jnp.float32) + taken[rows, :].astype(jnp.float32)
        ours += pair[rows, :].astype(jnp.float32)
        others = cross[rows, :].astype(jnp.float32) + far[rows, :].astype(jnp.float32)
        out[same[0]] = ours
        out[1 - same[0]] = others


def expert_outputs(same, own, taken, pair, cross, far):
    vmem = pl.BlockSpec(memory_space=pltpu.VMEM)
    first = pl.BlockSpec(memory_space=pl.ANY)
    return pl.pallas_call(
        expert_outputs_kernel,
        out_shape=(jax.ShapeDtypeStruct((CORES, HIDDEN, D), jnp.float32),) * 3,
        in_specs=[pl.BlockSpec(memory_space=pltpu.SMEM), vmem, first] + [vmem] * 3,
        out_specs=(vmem,) * 3,
        scratch_shapes=[pltpu.VMEM((3 * HIDDEN, D), jnp.bfloat16), pltpu.SemaphoreType.DMA],
        compiler_params=pltpu.CompilerParams(vmem_limit_bytes=VMEM_BYTES),
        cost_estimate=pl.CostEstimate(flops=0, bytes_accessed=20 << 20, transcendentals=0),
        name="expert_outputs",
    )(same, own, taken, pair, cross, far)


def kv_kernel(left, right, out):
    out[...] = jnp.dot(left[...], right[...], preferred_element_type=jnp.float32).astype(
        jnp.bfloat16
    )


def kv_product(left, right):
    vmem = pl.BlockSpec(memory_space=pltpu.VMEM)
    return pl.pallas_call(
        kv_kernel,
        out_shape=jax.ShapeDtypeStruct((left.shape[0], right.shape[1]), jnp.bfloat16),
        in_specs=[vmem] * 2,
        out_specs=vmem,
        compiler_params=pltpu.CompilerParams(vmem_limit_bytes=VMEM_BYTES),
        cost_estimate=pl.CostEstimate(flops=LONG, bytes_accessed=4 << 20, transcendentals=0),
        name="kv_product",
    )(left, right)


def attention_kernel(
    core, query_ref, compressed_ref, x_ref, factor_ref, w_query, w_down, kept, given, gain
):
    block = x_ref.shape[0] // (RINGS * CORES)

    def some(j, carry):
        columns = pl.ds(pl.multiple_of(j * WIDTH, WIDTH), WIDTH)
        scaled = x_ref[:, columns].astype(jnp.float32) * factor_ref[...]
        value = dot_nt(query_ref[...], w_query[columns, :])
        value += jnp.dot(
            compressed_ref[...], w_down[:, columns], preferred_element_type=jnp.float32
        )
        gain[:, columns] = jnp.sum(value * scaled, axis=0, keepdims=True)
        value = value.astype(jnp.bfloat16)
        for half in range(CORES):
            for target, chosen in ((kept, core[0] == half), (given, core[0] != half)):

                @pl.when(chosen)
                def _():
                    for chip in range(RINGS):
                        first = (chip * CORES + half) * block
                        target[chip * block : (chip + 1) * block, columns] = value[
                            first : first + block
                        ]

        return carry

    lax.fori_loop(0, D // WIDTH, some, 0)


def attention_rows(core, query, compressed, x, factor, w_query, w_down):
    half = jax.ShapeDtypeStruct((x.shape[0] // 2, D), jnp.bfloat16)
    vmem = pl.BlockSpec(memory_space=pltpu.VMEM)
    return pl.pallas_call(
        attention_kernel,
        out_shape=(half, half, jax.ShapeDtypeStruct((1, D), jnp.float32)),
        in_specs=[pl.BlockSpec(memory_space=pltpu.SMEM)] + [vmem] * 6,
        out_specs=(vmem,) * 3,
        compiler_params=pltpu.CompilerParams(vmem_limit_bytes=VMEM_BYTES),
        cost_estimate=pl.CostEstimate(flops=LONG, bytes_accessed=10 << 20, transcendentals=0),
        name="attention_rows",
    )(core, query, compressed, x, factor, w_query, w_down)


def expert_kernel(*refs):
    expert, x_hbm, y_hbm = refs[:3]
    blocks = refs[3:11]
    back, gate_out, up_out, act_out = refs[11:15]
    x_ref, y_ref, w_gate, w_up, w_down, sems = refs[15:]
    total = w_gate.shape[0]
    copies = [
        pltpu.make_async_copy(x_hbm, x_ref, sems.at[0]),
        pltpu.make_async_copy(y_hbm, y_ref, sems.at[1]),
    ]
    for i, block in enumerate(blocks):
        rows = pl.ds(i * HIDDEN, HIDDEN)
        for m, w in enumerate((w_gate, w_up, w_down)):
            copies.append(
                pltpu.make_async_copy(
                    block.at[pl.ds(m * HIDDEN, HIDDEN)], w.at[rows], sems.at[2 + 3 * i + m]
                )
            )
    for copy in copies:
        copy.start()
    half = 2 + len(copies[2:]) // 2
    for copy in copies[:half]:
        copy.wait()
    lanes = lax.broadcasted_iota(jnp.int32, (x_ref.shape[0], 128), 1)
    high_lane, low_lane = lanes == expert[0], lanes == expert[0] + LOW
    tail = x_ref[:, D:].astype(jnp.float32)
    gate = jnp.sum(jnp.where(high_lane | low_lane, tail, 0.0), axis=-1, keepdims=True)

    def hidden(start, width, summed):
        rows = pl.ds(start, width)
        x = x_ref[:, :D]
        gate_value = dot_nt(x, w_gate[rows, :])
        up_value = dot_nt(x, w_up[rows, :])
        raw = dot_nt(y_ref[...], w_down[rows, :])
        sigma = jax.nn.sigmoid(gate_value)
        swish = gate_value * sigma
        act = swish * up_value
        summed = summed + jnp.sum(raw * act, axis=-1, keepdims=True)
        raw = raw * gate
        slope = sigma * (1.0 + gate_value * (1.0 - sigma))
        gate_out[:, rows] = (raw * up_value * slope).astype(jnp.bfloat16)
        up_out[:, rows] = (raw * swish).astype(jnp.bfloat16)
        act_out[:, rows] = (act * gate).astype(jnp.bfloat16)
        return summed

    ready = (total // 2) // TILE
    whole = total // TILE
    summed = hidden_loop(0, ready, jnp.zeros((x_ref.shape[0], 1), jnp.float32), hidden)
    for copy in copies[half:]:
        copy.wait()
    summed = hidden_loop(ready, whole, summed, hidden)
    if total % TILE:
        summed = hidden(whole * TILE, total % TILE, summed)
    high = summed.astype(jnp.bfloat16).astype(jnp.float32)
    back[:, D:] = jnp.where(
        high_lane, high, jnp.where(low_lane, summed - high, 0.0)
    ).astype(jnp.bfloat16)

    def inward(j, carry):
        columns = pl.ds(pl.multiple_of(j * WIDTH, WIDTH), WIDTH)
        value = jnp.dot(gate_out[...], w_gate[:, columns], preferred_element_type=jnp.float32)
        value += jnp.dot(up_out[...], w_up[:, columns], preferred_element_type=jnp.float32)
        back[:, columns] = value.astype(jnp.bfloat16)
        return carry

    lax.fori_loop(0, D // WIDTH, inward, 0)


def expert_rows(expert, x, g_y, blocks):
    slots = x.shape[0]
    total = HIDDEN * len(blocks)
    bf16 = jnp.bfloat16
    anywhere = pl.BlockSpec(memory_space=pl.ANY)
    vmem = pl.BlockSpec(memory_space=pltpu.VMEM)
    return pl.pallas_call(
        expert_kernel,
        out_shape=(jax.ShapeDtypeStruct(x.shape, bf16),)
        + (jax.ShapeDtypeStruct((slots, total), bf16),) * 3,
        in_specs=[pl.BlockSpec(memory_space=pltpu.SMEM)] + [anywhere] * (2 + len(blocks)),
        out_specs=(vmem,) * 4,
        scratch_shapes=[
            pltpu.VMEM(x.shape, bf16),
            pltpu.VMEM((slots, D), bf16),
            pltpu.VMEM((total, D), bf16),
            pltpu.VMEM((total, D), bf16),
            pltpu.VMEM((total, D), bf16),
            pltpu.SemaphoreType.DMA((2 + 3 * len(blocks),)),
        ],
        compiler_params=pltpu.CompilerParams(vmem_limit_bytes=VMEM_BYTES),
        cost_estimate=pl.CostEstimate(
            flops=10 * slots * total * D, bytes_accessed=28 << 20, transcendentals=slots * total
        ),
        name="expert_rows",
    )(expert, x, g_y, *blocks)


def expert_weights_kernel(*refs):
    x_ref, y_ref, gate_ref, up_ref, act_ref = refs[:5]
    blocks = refs[5:13]
    out, places = refs[13], refs[14:19]
    w_down, holds, sems = refs[19], refs[20:23], refs[23]
    total = gate_ref.shape[1]
    loads = []
    for i, block in enumerate(blocks):
        loads.append(
            pltpu.make_async_copy(
                block.at[pl.ds(2 * HIDDEN, HIDDEN)],
                w_down.at[pl.ds(i * HIDDEN, HIDDEN)],
                sems.at[i],
            )
        )
        loads[-1].start()
    copies = []
    for m, (left, right) in enumerate(((gate_ref, x_ref), (up_ref, x_ref), (act_ref, y_ref))):

        def hidden(start, width, carry):
            rows = pl.ds(start, width)
            holds[m][rows, :] = dot_tn(left[:, rows], right[:, :D]).astype(jnp.bfloat16)
            return carry

        hidden_loop(0, total // TILE, 0, hidden)
        if total % TILE:
            hidden(total // TILE * TILE, total % TILE, 0)
        for i in range(len(blocks)):
            first = m + 3 * max(i - RINGS, 0)
            place = places[min(i, RINGS)].at[pl.ds(first * HIDDEN, HIDDEN)]
            source = holds[m].at[pl.ds(i * HIDDEN, HIDDEN)]
            copies.append(
                pltpu.make_async_copy(source, place, sems.at[len(blocks) * (m + 1) + i])
            )
            copies[-1].start()
    for load in loads:
        load.wait()

    def outward(j, carry):
        columns = pl.ds(pl.multiple_of(j * WIDTH, WIDTH), WIDTH)
        value = jnp.dot(act_ref[...], w_down[:, columns], preferred_element_type=jnp.float32)
        out[:, columns] = value.astype(jnp.bfloat16)
        return carry

    lax.fori_loop(0, D // WIDTH, outward, 0)
    for copy in copies:
        copy.wait()


def expert_weights(x, g_y, gate, up, act, blocks):
    slots, total = gate.shape
    bf16 = jnp.bfloat16
    anywhere = pl.BlockSpec(memory_space=pl.ANY)
    vmem = pl.BlockSpec(memory_space=pltpu.VMEM)
    sizes = (3 * HIDDEN,) * RINGS + (3 * HIDDEN * RINGS,)
    return pl.pallas_call(
        expert_weights_kernel,
        out_shape=(jax.ShapeDtypeStruct((slots, D), bf16),)
        + tuple(jax.ShapeDtypeStruct((size, D), bf16) for size in sizes),
        in_specs=[vmem] * 5 + [anywhere] * len(blocks),
        out_specs=(vmem,) + (anywhere,) * 5,
        scratch_shapes=[pltpu.VMEM((total, D), bf16)] * 4
        + [pltpu.SemaphoreType.DMA((4 * len(blocks),))],
        compiler_params=pltpu.CompilerParams(vmem_limit_bytes=VMEM_BYTES),
        cost_estimate=pl.CostEstimate(
            flops=LONG, bytes_accessed=34 << 20, transcendentals=0
        ),
        name="expert_weights",
    )(x, g_y, gate, up, act, *blocks)


def shards(
    layer_input,
    attn_gain,
    w_query,
    w_kv_down,
    kv_gain,
    w_kv_up,
    w_out,
    ffn_gain,
    w_router,
    routes,
    expert_gate,
    expert_up_projection,
    expert_down,
    shared_gate,
    shared_up,
    shared_down,
    cotangent,
):
    length = layer_input.shape[0]
    rows = length // (RINGS * CORES)
    y, core = lax.axis_index("y"), lax.axis_index("core")
    qk_width = NOPE + ROPE
    heads_here = w_query.shape[1] // qk_width
    score_scale = qk_width ** (-0.5)
    experts_total = w_router.shape[1]
    first_core = core == 0
    second_expert = y >= RINGS // 2

    def block_of(expert):
        parts = (
            jnp.swapaxes(expert_gate, 1, 2),
            jnp.swapaxes(expert_up_projection, 1, 2),
            expert_down,
        )
        return jnp.concatenate(
            [lax.dynamic_index_in_dim(part, expert, 0, keepdims=False) for part in parts], axis=0
        )

    same = second_expert.astype(jnp.int32)
    same_block, other_block = block_of(same), block_of(1 - same)
    weights = [
        same_block,
        lax.ppermute(same_block, "y", PAIRS),
        lax.ppermute(other_block, "y", CROSS),
    ]

    places = jnp.arange(length, dtype=jnp.int32)
    own_start = (y * CORES + core) * rows
    cot_all = gather_rows(cotangent)
    cot_rows = cotangent.astype(jnp.float32)

    def own(table):
        return lax.dynamic_slice_in_dim(table, own_start, rows, 0)

    def parts_of(table):
        return by_core(table, first_core)

    expert_ids = jnp.arange(experts_total, dtype=jnp.int32)
    picked = jnp.zeros((length, experts_total), jnp.float32)
    for route in range(TOP):
        picked = picked + (routes[:, route : route + 1] == expert_ids[None, :]).astype(jnp.float32)
    earlier = (places[:, None] > places[None, :]).astype(jnp.bfloat16)
    before = matmul(earlier, picked.astype(jnp.bfloat16))
    share = 128 // RINGS
    quarter = (y % 2) * CORES + core
    slots = jnp.arange(RANKS * share, dtype=jnp.int32)
    expert_of_slot = (experts_total // RANKS) * (slots // share) + same
    spread = (expert_ids[:, None] == expert_of_slot[None, :]).astype(jnp.bfloat16)
    place_of = matmul((picked * (before + 1.0)).astype(jnp.bfloat16), spread)
    slot_number = (slots % share + share * quarter + 1).astype(jnp.float32)
    slot_map = (place_of == slot_number[None, :]).astype(jnp.bfloat16)
    slot_parts = parts_of(slot_map)
    g_y_sent = matmul_tn(slot_map, cot_all).astype(jnp.bfloat16)
    g_y = to_owners(g_y_sent)

    cos_table, sin_table = angles_of(places)
    input_full = layer_input.astype(jnp.float32)
    normed_full, factor_one = norm_forward(input_full, attn_gain)
    normed_a = normed_full.astype(jnp.bfloat16)
    query_raw = matmul(normed_a, w_query).reshape(length, heads_here, qk_width)
    query_turned = rotate(query_raw[..., NOPE:], cos_table[:, None, :], sin_table[:, None, :])
    query = jnp.concatenate([query_raw[..., :NOPE], query_turned], axis=-1).astype(jnp.bfloat16)
    compressed = matmul(normed_a, w_kv_down)
    latent_raw = compressed[:, :KV_RANK]
    latent_normed, factor_kv = norm_forward(latent_raw, kv_gain)
    latent = latent_normed.astype(jnp.bfloat16)
    key_rope = rotate(compressed[:, KV_RANK:], cos_table, sin_table).astype(jnp.bfloat16)
    key_value = (
        matmul(latent, w_kv_up).astype(jnp.bfloat16).reshape(length, heads_here, NOPE + VDIM)
    )
    key_nope = key_value[..., :NOPE]
    values_all = key_value[..., NOPE:]
    causal = places[:, None] >= places[None, :]

    def scores_of(query):
        scores = jnp.einsum(
            "qhd,khd->hqk", query[..., :NOPE], key_nope, preferred_element_type=jnp.float32
        )
        scores = scores + jnp.einsum(
            "qhd,kd->hqk", query[..., NOPE:], key_rope, preferred_element_type=jnp.float32
        )
        return jnp.where(causal[None], scores * score_scale, -1e30)

    scores = scores_of(query)
    top_score = jnp.max(scores, axis=-1, keepdims=True)
    powered = jnp.exp(scores - top_score)
    total = jnp.sum(powered, axis=-1, keepdims=True)
    probs = (powered / total).astype(jnp.bfloat16)
    log_totals = top_score + jnp.log(total)
    heads_out = (
        jnp.einsum("hqk,khd->qhd", probs, values_all, preferred_element_type=jnp.float32)
        .astype(jnp.bfloat16)
        .reshape(length, heads_here * VDIM)
    )
    attn_kept, attn_given = parts_of(matmul(heads_out, w_out).astype(jnp.bfloat16))
    attended = sum_rows_directly(after(attn_kept, g_y_sent, *weights[1:]), attn_given)
    residual = own(input_full) + attended
    normed_two, factor_two = norm_forward(residual, ffn_gain)
    normed_rows = normed_two.astype(jnp.bfloat16)
    normed_f = gather_rows(normed_rows)
    weights.append(lax.ppermute(after(other_block, normed_f), "y", OPPOSITE))

    sigmoid_all = jax.nn.sigmoid(matmul(normed_f, w_router))
    selected = sigmoid_all * picked
    sel_total = jnp.sum(selected, axis=-1, keepdims=True)
    gates = route_scale * selected / sel_total
    high, low = split_float(gates)
    gap = jnp.zeros((length, LOW - experts_total), jnp.bfloat16)
    sent = dispatch(slot_map, normed_f, jnp.concatenate([high, gap, low, gap], axis=1))
    arrived = to_owners(after(sent, g_y))

    core_index = core.reshape(1).astype(jnp.int32)
    *grads_shared, shared_act, kept_back, given_back = shared_experts(
        core_index,
        after(normed_f, sent),
        cot_all,
        jnp.swapaxes(shared_gate, 0, 1),
        jnp.swapaxes(shared_up, 0, 1),
        shared_down,
    )

    shared_back = (kept_back, given_back)

    arrived = after(arrived, *shared_back)
    last = after(weights[-1], arrived)
    weights = weights + [lax.ppermute(w, "core", SWAP) for w in (*weights[:-1], last)]
    expert_here = 2 * lax.axis_index("x") * 4 + 2 * lax.axis_index("z") + same
    back, g_gate, g_up, act = expert_rows(
        expert_here.reshape(1).astype(jnp.int32), arrived, g_y, weights
    )
    out, *block_grads = expert_weights(
        arrived, g_y, g_gate, g_up, act, weights
    )
    back = after(to_owners(back), *block_grads)

    taken_grads = lax.ppermute(block_grads[RINGS], "core", SWAP)

    summed = sum_rows_directly(
        *(
            matmul(a, back) + jnp.pad(b, ((0, 0), (0, 128)))
            for a, b in zip(slot_parts, shared_back)
        )
    )
    g_gate_rows = summed[:, D : D + experts_total] + summed[:, D + LOW : D + LOW + experts_total]

    sigma_rows, picked_rows, total_rows = own(sigmoid_all), own(picked), own(sel_total)
    sel_rows = sigma_rows * picked_rows
    grad_sel = route_scale * (
        g_gate_rows / total_rows
        - jnp.sum(g_gate_rows * sel_rows, axis=-1, keepdims=True) / (total_rows * total_rows)
    )
    grad_logits = (grad_sel * picked_rows * sigma_rows * (1.0 - sigma_rows)).astype(jnp.bfloat16)
    grad_w_router = matmul_tn(grad_logits, normed_rows)
    grad_normed = summed[:, :D] + matmul_nt(grad_logits, w_router)
    grad_from_norm, grad_ffn_gain = norm_backward(residual, factor_two, ffn_gain, grad_normed)
    grad_residual = cot_rows + grad_from_norm
    grad_residual_low = grad_residual.astype(jnp.bfloat16)
    grad_attended = gather_rows(grad_residual_low)
    returned = to_owners(after(out, grad_residual_low))

    grad_w_out = matmul_tn(heads_out, grad_attended).astype(jnp.bfloat16)

    grad_heads = (
        matmul_nt(grad_attended, w_out).astype(jnp.bfloat16).reshape(length, heads_here, VDIM)
    )
    probs_full = jnp.exp(scores_of(query) - log_totals)
    grad_probs = jnp.einsum(
        "qhd,khd->hqk", grad_heads, values_all, preferred_element_type=jnp.float32
    )
    grad_scores = (
        probs_full * (grad_probs - jnp.sum(grad_probs * probs_full, axis=-1, keepdims=True))
    ).astype(jnp.bfloat16)
    grad_query_nope = (
        jnp.einsum("hqk,khd->qhd", grad_scores, key_nope, preferred_element_type=jnp.float32)
        * score_scale
    )
    grad_query_rope = (
        jnp.einsum("hqk,kd->qhd", grad_scores, key_rope, preferred_element_type=jnp.float32)
        * score_scale
    )
    grad_key_nope = (
        jnp.einsum(
            "hqk,qhd->khd", grad_scores, query[..., :NOPE], preferred_element_type=jnp.float32
        )
        * score_scale
    )
    grad_key_rope = (
        jnp.einsum(
            "hqk,qhd->kd", grad_scores, query[..., NOPE:], preferred_element_type=jnp.float32
        )
        * score_scale
    )
    grad_values = jnp.einsum(
        "hqk,qhd->khd",
        probs_full.astype(jnp.bfloat16),
        grad_heads,
        preferred_element_type=jnp.float32,
    )
    grad_query_back = rotate_back(
        grad_query_rope, cos_table[:, None, :], sin_table[:, None, :]
    )
    grad_query = (
        jnp.concatenate([grad_query_nope, grad_query_back], axis=-1)
        .astype(jnp.bfloat16)
        .reshape(length, heads_here * qk_width)
    )
    grad_w_query = matmul_tn(normed_a, grad_query).astype(jnp.bfloat16)
    grad_key_value = (
        jnp.concatenate([grad_key_nope, grad_values], axis=-1)
        .astype(jnp.bfloat16)
        .reshape(length, heads_here * (NOPE + VDIM))
    )
    grad_w_kv_up = matmul_tn(latent, grad_key_value).astype(jnp.bfloat16)
    grad_latent_normed = matmul_nt(grad_key_value, w_kv_up)
    grad_latent, grad_kv_gain = norm_backward(latent_raw, factor_kv, kv_gain, grad_latent_normed)
    grad_rope_part = rotate_back(grad_key_rope, cos_table, sin_table)
    grad_compressed = jnp.concatenate([grad_latent, grad_rope_part], axis=-1).astype(jnp.bfloat16)
    local_grads = (grad_w_out, grad_w_query, grad_w_kv_up, *grads_shared)
    grad_w_out, grad_w_query, grad_w_kv_up, *grads_shared = lax.psum(local_grads, EXPERT)
    kept, given, grad_attn_gain = attention_rows(
        core_index,
        grad_query,
        grad_compressed,
        layer_input,
        factor_one,
        w_query,
        jnp.swapaxes(w_kv_down, 0, 1),
    )

    parts = RINGS * CORES
    kv_share = grad_compressed.shape[1] // parts
    columns = D // parts
    gains = jnp.concatenate(
        [
            grad_attn_gain.reshape(parts, columns),
            grad_ffn_gain.reshape(parts, columns),
            grad_kv_gain.reshape(parts, KV_RANK // parts),
        ],
        axis=1,
    )
    gains = jnp.pad(gains, ((0, 0), (0, 16 * length // 2 - gains.shape[1])))
    bundle = jnp.concatenate(
        [
            jnp.swapaxes(grad_compressed, 0, 1).reshape(parts, kv_share, length),
            jnp.swapaxes(grad_w_router.reshape(experts_total, parts, columns), 0, 1)
            .reshape(parts, experts_total * columns // length, length)
            .astype(jnp.bfloat16),
            gains.reshape(parts, 8, length).astype(jnp.bfloat16),
        ],
        axis=1,
    )
    bundle = after(bundle, returned, *local_grads)

    def last_sums():
        grads_sent, taken = [], taken_grads
        for r in range(1, RINGS):
            part = taken[3 * HIDDEN * r : 3 * HIDDEN * (r + 1)].astype(jnp.float32)
            grads_sent.append((block_grads[r].astype(jnp.float32) + part).astype(jnp.bfloat16))
            taken = after(taken_grads, grads_sent[-1])
        tiles = lax.all_to_all(bundle, GROUP, 0, 0, tiled=True)
        slices = total_of(tiles).astype(jnp.bfloat16)
        pair_grads = lax.ppermute(grads_sent[0], "y", PAIRS)
        cross_grads = lax.ppermute(grads_sent[1], "y", CROSS)
        act_parts = parts_of(shared_act)
        both_sums = sum_rows_directly(
            *(
                jnp.concatenate(
                    [c, (matmul(a, returned) + matmul(b, shared_down)).astype(jnp.bfloat16)], axis=1
                )
                for a, b, c in zip(slot_parts, act_parts, (kept, given))
            )
        )
        grad_normed_one, routed_and_shared = both_sums[:, :D], both_sums[:, D:]
        output = (residual + routed_and_shared).astype(jnp.bfloat16)
        grad_from_first, _ = norm_backward(
            own(input_full), own(factor_one), attn_gain, grad_normed_one
        )
        grad_input = grad_residual + grad_from_first
        far_grads = lax.ppermute(
            after(grads_sent[2], slices), "y", OPPOSITE
        )
        kv_slice = kv_product(slices[:kv_share], normed_a)
        other_rows = slices[kv_share:].reshape(-1, D)
        rest = jnp.zeros((80 - kv_share - other_rows.shape[0], D), jnp.bfloat16)
        replicated = jnp.concatenate([kv_slice, other_rows, rest], axis=0)
        replicated = jnp.swapaxes(replicated.reshape(80, RANKS, D // RANKS), 0, 1)
        replicated = sum_ranks(replicated)
        expert_grads = expert_outputs(
            same.reshape(1), block_grads[0], taken_grads, pair_grads, cross_grads, far_grads
        )
        replicated = after(
            replicated, pair_grads
        )
        replicated = gather_rows_directly(
            replicated.reshape(RANKS * 80, D // RANKS), first_core, expert_grads
        )
        return grad_input, replicated, output, expert_grads

    grad_input, replicated, output, expert_grads = as_unit(
        last_sums, routes[0, 0] >= 0
    )
    replicated = replicated.reshape(parts, RANKS, 80, D // RANKS)

    def unpacked(first, last):
        piece = jnp.swapaxes(replicated[:, :, first:last], 1, 2)
        return piece.reshape(parts, last - first, D).astype(jnp.float32)

    grad_w_kv_down = jnp.swapaxes(unpacked(0, kv_share).reshape(-1, D), 0, 1)
    router_rows = experts_total * columns // D
    grad_w_router = (
        jnp.swapaxes(
            unpacked(kv_share, kv_share + router_rows).reshape(parts, experts_total, columns), 0, 1
        )
        .reshape(experts_total, D)
        .T
    )
    gains = unpacked(kv_share + router_rows, kv_share + router_rows + 1)[:, 0]
    grad_attn_gain = gains[:, :columns].reshape(D)
    grad_ffn_gain = gains[:, columns : 2 * columns].reshape(D)
    grad_kv_gain = gains[:, 2 * columns : 2 * columns + KV_RANK // parts].reshape(KV_RANK)
    grads_shared = [grad.astype(jnp.float32) for grad in grads_shared]
    return (
        output,
        grad_input,
        grad_attn_gain,
        grad_w_query.astype(jnp.float32),
        grad_w_kv_down,
        grad_kv_gain,
        grad_w_kv_up.astype(jnp.float32),
        grad_w_out.astype(jnp.float32),
        grad_ffn_gain,
        grad_w_router,
        jnp.swapaxes(expert_grads[0], 1, 2),
        jnp.swapaxes(expert_grads[1], 1, 2),
        expert_grads[2],
        grads_shared[0].T,
        grads_shared[1].T,
        grads_shared[2],
    )


def solution(mesh):
    split = Mesh(mesh.devices.reshape(4, 4, RINGS, CORES), ("x", "z", "y", "core"))
    return jax.shard_map(
        shards,
        mesh=split,
        in_specs=(
            P(EXPERT, None),
            P(),
            P(None, GROUP),
            P(),
            P(),
            P(None, GROUP),
            P(GROUP, None),
            P(),
            P(),
            P(EXPERT, None),
            P(EXPERT, None, GROUP),
            P(EXPERT, None, GROUP),
            P(EXPERT, GROUP, None),
            P(None, GROUP),
            P(None, GROUP),
            P(GROUP, None),
            P(("x", "z", "y", "core"), None),
        ),
        out_specs=(
            P(("x", "z", "y", "core"), None),
            P(("x", "z", "y", "core"), None),
            P(),
            P(None, GROUP),
            P(),
            P(),
            P(None, GROUP),
            P(GROUP, None),
            P(),
            P(),
            P(EXPERT, None, GROUP),
            P(EXPERT, None, GROUP),
            P(EXPERT, GROUP, None),
            P(None, GROUP),
            P(None, GROUP),
            P(GROUP, None),
        ),
        check_vma=False,
    )
```
